32 devices in a mesh: row: 4 (over y, x), col: 8 (over z, core).
Axes of the slice: x: 2, y: 2, z: 4, core: 2. Of those that a mesh axis runs over, the one named last changes fastest.
Arguments:
- window: float32 [12288, 12288], P('row', 'col'), may hold values from -6 to 6
- reflectors: float32 [2, 12288, 256], P(None, 'row', 'col'), may hold values from -0.0546875 to 0.0546875
- factors: float32 [2, 256, 256], replicated, may hold values from -0.375 to 0.375
Outputs:
- updated: float32 [12288, 12288], P('row', 'col')
The draws below stay inside these ranges and needn't reach their ends.
All inputs are finite; a program needn't handle non-finite values.
Results may differ from the reference program's by a relative error of at most 0.0001.
Values sent between devices are 32-bit elements; how exact they have to be, the bound alone decides.
No kernel may reach another device: no remote copies, remote signals or barrier semaphores. Data moves between devices by JAX's collectives and lax.ppermute only.
A program may use at most 128 MiB of HBM per device.

```python
import jax
import jax.numpy as jnp
from jax import lax

N = 12288
B = 256
PANELS = 2


def block_levels(key, dims, shards, least, largest):
    level = 1.0
    for dim, blocks in shards:
        steps = jax.random.uniform(jax.random.fold_in(jax.random.fold_in(key, 6), dim), (blocks,), jnp.float32, least / len(shards), largest / len(shards))
        level = level * jnp.repeat(jnp.exp(steps), dims[dim] // blocks).reshape((-1,) + (1,) * (len(dims) - 1 - dim))
    return level


def gaussian(own_key, dims, spread, bound, pieces=(), held_as=jnp.bfloat16):
    level = block_levels(own_key, dims, pieces, -0.22, 0.18) if pieces else 1.0
    result = jax.random.normal(own_key, dims, jnp.float32) * spread * level
    return jnp.minimum(jnp.maximum(result, -bound), bound).astype(held_as)


def setup_inputs(seed: int = 0) -> dict:
    streams_of = jax.random.split(jax.random.key(seed), 4)
    window = gaussian(streams_of[0], (N, N), 1.0, 6.0, ((0, 4), (1, 8)), jnp.float32)
    reflectors = gaussian(streams_of[1], (PANELS, N, B), N ** -0.5, 0.0546875, ((1, 4), (2, 8)), jnp.float32)
    factors = gaussian(streams_of[2], (PANELS, B, B), B ** -0.5, 0.375, (), jnp.float32)
    return {"window": window, "reflectors": reflectors, "factors": factors}


highest = lax.Precision.HIGHEST


def product(factor_one, factor_two):
    return jnp.dot(factor_one, factor_two, precision=highest, preferred_element_type=jnp.float32)


def reference(window, reflectors, factors):
    updated = window
    for panel in range(PANELS):
        vectors = reflectors[panel]
        factor = factors[panel]
        projected = product(vectors.T, updated)
        updated = updated - product(vectors, product(factor.T, projected))
        image = product(updated, vectors)
        updated = updated - product(product(image, factor), vectors.T)
    return updated
```

```python
import functools

import jax
import jax.numpy as jnp
from jax import lax
from jax.experimental import pallas as pl
from jax.experimental.pallas import tpu as pltpu
from jax.sharding import PartitionSpec as P

f32 = jnp.float32
bf16 = jnp.bfloat16
VMEM_BYTES = 50 * 1024 * 1024


def halves(value):
    high = value.astype(bf16)
    return high, (value - high.astype(f32)).astype(bf16)


def dot(one, two, one_dim=1, two_dim=0):
    return lax.dot_general(
        one, two, (((one_dim,), (two_dim,)), ((), ())), preferred_element_type=f32
    )


def small(one, two, one_dim=1, two_dim=0):
    return lax.dot_general(
        one,
        two,
        (((one_dim,), (two_dim,)), ((), ())),
        precision=lax.Precision.HIGH,
        preferred_element_type=f32,
    )


def call(kernel, grid, in_specs, out_specs, out_shape, scratch, flops, nbytes):
    return pl.pallas_call(
        kernel,
        grid=grid,
        in_specs=in_specs,
        out_specs=out_specs,
        out_shape=out_shape,
        scratch_shapes=scratch,
        compiler_params=pltpu.CompilerParams(vmem_limit_bytes=VMEM_BYTES),
        cost_estimate=pl.CostEstimate(flops=flops, bytes_accessed=nbytes, transcendentals=0),
    )


def project_kernel(vectors_ref, window_ref, out_ref, both_ref):
    width = vectors_ref.shape[0]

    @pl.when(pl.program_id(0) == 0)
    def _():
        high, low = halves(vectors_ref[...])
        both_ref[:width] = high
        both_ref[width:] = low

    high, low = halves(window_ref[...])
    first = dot(both_ref[...], high)
    out_ref[...] = first[:width] + first[width:] + dot(both_ref[:width], low)


def project(vectors, window, block=256):
    width, rows = vectors.shape
    cols = window.shape[1]
    return call(
        project_kernel,
        (cols // block,),
        [
            pl.BlockSpec((width, rows), lambda i: (0, 0)),
            pl.BlockSpec((rows, block), lambda i: (0, i)),
        ],
        pl.BlockSpec((width, block), lambda i: (0, i)),
        jax.ShapeDtypeStruct((width, cols), f32),
        [pltpu.VMEM((2 * width, rows), bf16)],
        6 * width * rows * cols,
        4 * (rows * cols + width * (rows + cols)),
    )(vectors, window)


def image_kernel(window_ref, vectors_ref, out_ref, both_ref):
    width = vectors_ref.shape[0]

    @pl.when(pl.program_id(0) == 0)
    def _():
        high, low = halves(vectors_ref[...])
        both_ref[:width] = high
        both_ref[width:] = low

    high, low = halves(window_ref[...])
    first = dot(high, both_ref[...], 1, 1)
    out_ref[...] = first[:, :width] + first[:, width:] + dot(low, both_ref[:width], 1, 1)


def image(window, vectors, block=512):
    rows, cols = window.shape
    width = vectors.shape[0]
    block = min(block, rows)
    return call(
        image_kernel,
        (rows // block,),
        [
            pl.BlockSpec((block, cols), lambda i: (i, 0)),
            pl.BlockSpec((width, cols), lambda i: (0, 0)),
        ],
        pl.BlockSpec((block, width), lambda i: (i, 0)),
        jax.ShapeDtypeStruct((rows, width), f32),
        [pltpu.VMEM((2 * width, cols), bf16)],
        6 * width * rows * cols,
        4 * (rows * cols + width * (rows + cols)),
    )(window, vectors)


def subtract_kernel(flip, window_ref, left_ref, right_ref, out_ref, high_ref, low_ref):
    @pl.when(pl.program_id(0) == 0)
    def _():
        high_ref[...], low_ref[...] = halves(right_ref[...])

    left = left_ref[...].T if flip else left_ref[...]
    high, low = halves(left)
    out_ref[...] = window_ref[...] - (
        dot(high, high_ref[...]) + (dot(high, low_ref[...]) + dot(low, high_ref[...]))
    )


def subtract(window, left, right, flip=False, block=512):
    rows, cols = window.shape
    width = right.shape[0]
    block = min(block, rows)
    if flip:
        left_spec = pl.BlockSpec((width, block), lambda i: (0, i))
    else:
        left_spec = pl.BlockSpec((block, width), lambda i: (i, 0))
    return call(
        functools.partial(subtract_kernel, flip),
        (rows // block,),
        [
            pl.BlockSpec((block, cols), lambda i: (i, 0)),
            left_spec,
            pl.BlockSpec((width, cols), lambda i: (0, 0)),
        ],
        pl.BlockSpec((block, cols), lambda i: (i, 0)),
        jax.ShapeDtypeStruct((rows, cols), f32),
        [pltpu.VMEM((width, cols), bf16)] * 2,
        6 * width * rows * cols,
        4 * (2 * rows * cols + width * (rows + cols)),
    )(window, left, right)


def spread(value, row_count, col_count):
    bits = [1 << bit for bit in range(row_count.bit_length() - 1)]
    row_index = lax.axis_index("row")
    col_index = lax.axis_index("col")
    distance = row_index ^ (col_index * row_count // col_count)
    results = []
    middle = value.shape[0] // 2
    for part, order in ((value[:middle], bits), (value[middle:], bits[::-1])):
        have = [0]
        for bit in order:
            pairs = []
            for col in range(col_count):
                source = col * row_count // col_count
                for offset in have:
                    pairs.append(
                        (
                            (source ^ offset) * col_count + col,
                            (source ^ offset ^ bit) * col_count + col,
                        )
                    )
            arrived = lax.ppermute(part, ("row", "col"), pairs)
            takes = functools.reduce(jnp.logical_or, [distance == offset ^ bit for offset in have])
            part = jnp.where(takes, arrived, part)
            have += [offset ^ bit for offset in have]
        results.append(part)
    return jnp.concatenate(results, 0)


def body(window, reflectors, factors):
    row_count = lax.axis_size("row")
    col_count = lax.axis_size("col")
    row_index = lax.axis_index("row")
    col_index = lax.axis_index("col")
    rows, cols = window.shape
    panels = reflectors.shape[0]
    slivers = jnp.swapaxes(reflectors, 1, 2)
    offset = (col_index * cols) % rows

    row_vectors, col_vectors, projected, images = [], [], [], []
    for panel in range(panels):
        vectors = lax.all_gather(slivers[panel], "col", axis=0, tiled=True)
        row_vectors.append(vectors)
        mine = lax.dynamic_slice_in_dim(vectors, offset, cols, 1)
        col_vectors.append(spread(mine, row_count, col_count))
    for panel in range(panels):
        projected.append(project(row_vectors[panel], window))
        images.append(image(window, col_vectors[panel]))
    row_all = jnp.concatenate(row_vectors, 0)
    col_all = jnp.concatenate(col_vectors, 0)
    projected = jnp.concatenate(projected, 0)
    crossed = small(projected, col_all, 1, 1)
    share = rows // col_count
    part = lax.dynamic_slice_in_dim(row_all, col_index * share, share, 1)
    inner = small(part, part, 1, 1)
    crossed, inner = lax.psum((crossed, inner), ("row", "col"))
    projected = lax.psum(projected, "row")
    images = [lax.psum(value, "col") for value in images]

    width = row_vectors[0].shape[0]
    joined = factors[0]
    for panel in range(1, panels):
        done = panel * width
        factor = factors[panel]
        between = -small(joined, small(inner[:done, done : done + width], factor))
        joined = jnp.block([[joined, between], [jnp.zeros((width, done), f32), factor]])
    right = small(joined, col_all)
    left = small(joined, projected - small(crossed, right), 0, 0)
    updated = subtract(window, row_all, left, flip=True)
    for panel in range(panels):
        updated = subtract(updated, images[panel], right[panel * width : (panel + 1) * width])
    return updated


def solution(mesh):
    placed = (P("row", "col"), P(None, "row", "col"), P())
    return jax.shard_map(
        body, mesh=mesh, in_specs=placed, out_specs=P("row", "col"), check_vma=False
    )
```

```python
import functools

import jax
import jax.numpy as jnp
from jax import lax
from jax.experimental import pallas as pl
from jax.experimental.pallas import tpu as pltpu
from jax.sharding import PartitionSpec as P

f32 = jnp.float32
bf16 = jnp.bfloat16
VMEM_BYTES = 50 * 1024 * 1024


def halves(value):
    high = value.astype(bf16)
    return high, (value - high.astype(f32)).astype(bf16)


def dot(one, two, one_dim=1, two_dim=0):
    return lax.dot_general(
        one, two, (((one_dim,), (two_dim,)), ((), ())), preferred_element_type=f32
    )


def small(one, two, one_dim=1, two_dim=0):
    return lax.dot_general(
        one,
        two,
        (((one_dim,), (two_dim,)), ((), ())),
        precision=lax.Precision.HIGH,
        preferred_element_type=f32,
    )


def call(kernel, grid, in_specs, out_specs, out_shape, scratch=(), aliases=None):
    return pl.pallas_call(
        kernel,
        grid=grid,
        in_specs=in_specs,
        out_specs=out_specs,
        out_shape=out_shape,
        scratch_shapes=scratch,
        input_output_aliases=aliases or {},
        compiler_params=pltpu.CompilerParams(vmem_limit_bytes=VMEM_BYTES),
        cost_estimate=pl.CostEstimate(flops=1, bytes_accessed=1, transcendentals=0),
    )


def project_kernel(vectors_ref, window_ref, out_ref, both_ref):
    width = vectors_ref.shape[0]

    @pl.when(pl.program_id(0) == 0)
    def _():
        high, low = halves(vectors_ref[...])
        both_ref[:width] = high
        both_ref[width:] = low

    high, low = halves(window_ref[...])
    first = dot(both_ref[...], high)
    out_ref[...] = first[:width] + first[width:] + dot(both_ref[:width], low)


def project(vectors, window, block=256):
    width, rows = vectors.shape
    cols = window.shape[1]
    return call(
        project_kernel,
        (cols // block,),
        [
            pl.BlockSpec((width, rows), lambda i: (0, 0)),
            pl.BlockSpec((rows, block), lambda i: (0, i)),
        ],
        pl.BlockSpec((width, block), lambda i: (0, i)),
        jax.ShapeDtypeStruct((width, cols), f32),
        [pltpu.VMEM((2 * width, rows), bf16)],
    )(vectors, window)


def image_kernel(window_ref, vectors_ref, out_ref, both_ref):
    width = vectors_ref.shape[0]

    @pl.when(pl.program_id(0) == 0)
    def _():
        high, low = halves(vectors_ref[...])
        both_ref[:width] = high
        both_ref[width:] = low

    high, low = halves(window_ref[...])
    first = dot(high, both_ref[...], 1, 1)
    out_ref[...] = first[:, :width] + first[:, width:] + dot(low, both_ref[:width], 1, 1)


def image(window, vectors, block=512):
    rows, cols = window.shape
    width = vectors.shape[0]
    block = min(block, rows)
    return call(
        image_kernel,
        (rows // block,),
        [
            pl.BlockSpec((block, cols), lambda i: (i, 0)),
            pl.BlockSpec((width, cols), lambda i: (0, 0)),
        ],
        pl.BlockSpec((block, width), lambda i: (i, 0)),
        jax.ShapeDtypeStruct((rows, width), f32),
        [pltpu.VMEM((2 * width, cols), bf16)],
    )(window, vectors)


def three_products(high, low, high_ref, low_ref):
    return dot(high, high_ref[...]) + (dot(high, low_ref[...]) + dot(low, high_ref[...]))


def update_kernel(window_ref, near_ref, far_ref, high_ref, low_ref, out_ref):
    vectors = jnp.concatenate([near_ref[...].T, far_ref[...].T], 1)
    out_ref[...] = window_ref[...] - three_products(*halves(vectors), high_ref, low_ref)


def update(window, near, far, high, low, block=512):
    rows, cols = window.shape
    part, width = near.shape[0], high.shape[0]
    block = min(block, rows)
    return call(
        update_kernel,
        (rows // block,),
        [
            pl.BlockSpec((block, cols), lambda i: (i, 0)),
            pl.BlockSpec((part, block), lambda i: (0, i)),
            pl.BlockSpec((part, block), lambda i: (0, i)),
            pl.BlockSpec((width, cols), lambda i: (0, 0)),
            pl.BlockSpec((width, cols), lambda i: (0, 0)),
        ],
        pl.BlockSpec((block, cols), lambda i: (i, 0)),
        jax.ShapeDtypeStruct((rows, cols), f32),
    )(window, near, far, high, low)


def finish_kernel(
    window_ref, near_ref, far_ref, middle_high, middle_low, high_ref, low_ref, *refs
):
    vectors = jnp.concatenate([near_ref[...].T, far_ref[...].T], 1)
    *image_refs, out_ref = refs
    images = jnp.concatenate([one[...] for one in image_refs], 1)
    left = images - three_products(*halves(vectors), middle_high, middle_low)
    out_ref[...] = window_ref[...] - three_products(*halves(left), high_ref, low_ref)


def finish(window, near, far, images, middle, right, block=512):
    rows, cols = window.shape
    part, width = near.shape[0], right[0].shape[0]
    block = min(block, rows)
    return call(
        finish_kernel,
        (rows // block,),
        [
            pl.BlockSpec((block, cols), lambda i: (i, 0)),
            pl.BlockSpec((part, block), lambda i: (0, i)),
            pl.BlockSpec((part, block), lambda i: (0, i)),
            pl.BlockSpec((width, width), lambda i: (0, 0)),
            pl.BlockSpec((width, width), lambda i: (0, 0)),
            pl.BlockSpec((width, cols), lambda i: (0, 0)),
            pl.BlockSpec((width, cols), lambda i: (0, 0)),
        ]
        + [pl.BlockSpec((block, one.shape[1]), lambda i: (i, 0)) for one in images],
        pl.BlockSpec((block, cols), lambda i: (i, 0)),
        jax.ShapeDtypeStruct((rows, cols), f32),
        aliases={0: 0},
    )(window, near, far, *middle, *right, *images)


def swap_cores(value):
    count = lax.axis_size("col")
    return lax.ppermute(value, "col", [(col, col ^ 1) for col in range(count)])


def swap_chips(value, distance):
    count = lax.axis_size("col")
    return lax.ppermute(value, "col", [(col, col ^ (2 * distance)) for col in range(count)])


def swap_rows(value, distance):
    count = lax.axis_size("row")
    return lax.ppermute(value, "row", [(row, row ^ distance) for row in range(count)])


def at(value, index, dim):
    return lax.dynamic_index_in_dim(value, index, dim, keepdims=False)


def put(whole, value, index, dim):
    return lax.dynamic_update_slice_in_dim(whole, jnp.expand_dims(value, dim), index, dim)


def together(*values):
    return lax.optimization_barrier(values)


def region(run, *operands):
    results = jax.eval_shape(run, *operands)

    def nothing(*_):
        return jax.tree.map(lambda one: jnp.zeros(one.shape, one.dtype), results)

    return lax.cond(lax.axis_index("col") >= 0, run, nothing, *operands)


def ordered(condition, one, two, dim):
    return jnp.concatenate([jnp.where(condition, one, two), jnp.where(condition, two, one)], dim)


def by_chip(choose):
    chip = lax.axis_index("col") // 2
    value = choose(0)
    for one in range(1, lax.axis_size("col") // 2):
        value = jnp.where(chip == one, choose(one), value)
    return value


def send_along(value, chips, step, count=None):
    count = chips if count is None else count
    ends = range(count) if step < 0 else range(chips - count, chips)
    return lax.ppermute(
        value,
        "col",
        [
            (2 * (chip - step) + core, 2 * chip + core)
            for chip in ends
            for core in range(2)
            if 0 <= chip - step < chips
        ],
    )


def both_cores(mine, other):
    core = lax.axis_index("col") % 2
    pairs = []
    for place in range(mine.shape[1]):
        one, two = mine[:, place], other[:, place]
        pairs += [jnp.where(core == 0, one, two), jnp.where(core == 0, two, one)]
    return jnp.concatenate(pairs, 1).reshape(-1, mine.shape[-1])


def gather_vectors(slivers, row_count, chips, window):
    col_index, row = lax.axis_index("col"), lax.axis_index("row")
    core, chip = col_index % 2, col_index // 2
    panels, piece, rows = slivers.shape
    cols = rows // 2
    share = 2 * piece // row_count
    distances = range(1, row_count)
    half = chips // 2

    mine = lax.dynamic_slice_in_dim(slivers, core * cols, cols, 2)
    other = swap_cores(lax.dynamic_slice_in_dim(slivers, (1 - core) * cols, cols, 2))
    shares = ordered(core == 0, mine, other, 1).reshape(panels, row_count, share, cols)
    arrived = [swap_rows(at(shares, row ^ distance, 1), distance) for distance in distances]
    held = {0: slivers}
    for step in range(1, half):
        after, before, *arrived = together(
            send_along(held[step - 1], chips, -1), send_along(held[1 - step], chips, 1), *arrived
        )
        held[step], held[-step] = after, before
    by_row = jnp.zeros((panels, row_count, share, cols), f32)
    by_row = put(by_row, at(shares, row, 1), row, 1)
    for distance, value in zip(distances, arrived):
        by_row = put(by_row, value, row ^ distance, 1)

    near = jnp.stack(
        [by_chip(lambda one: held[one // half * half + place - one]) for place in range(half)], 1
    )

    def along_line(panel):
        return [swap_chips(at(by_row[panel], chip ^ distance, 0), distance) for distance in distances]

    def line_shares(panel, arrived):
        shares = jnp.zeros((row_count, share, cols), f32)
        shares = put(shares, at(by_row[panel], chip, 0), chip, 0)
        for distance, value in zip(distances, arrived):
            shares = put(shares, value, chip ^ distance, 0)
        return shares

    def all_rows(shares, arrived):
        whole = jnp.zeros((row_count, row_count, share, cols), f32)
        whole = put(whole, shares, row, 1)
        for distance, value in zip(distances, arrived):
            whole = put(whole, value, row ^ distance, 1)
        return whole.reshape(2 * chips * piece, cols)

    other, arrived = together(swap_cores(near), along_line(0))
    near = both_cores(near, other)
    shares = [line_shares(0, arrived)]
    last = (held[half - 1], held[1 - half])
    *last, near, shares[0] = together(*last, near, shares[0])

    columns, images = [], []
    for panel in range(panels):
        arrived = [swap_rows(shares[panel], distance) for distance in distances]
        following = along_line(panel + 1) if panel + 1 < panels else []
        if panel == 0:
            projected, arrived, following = together(project(near, window), arrived, following)
        else:
            jumps = range(1, half)
            after = [send_along(last[0], chips, -jump, chips - half - jump + 1) for jump in jumps]
            before = [send_along(last[1], chips, jump, chips - half - jump + 1) for jump in jumps]
            images.append(image(window, columns[-1]))
            images[-1], arrived, following, after, before = together(
                images[-1], arrived, following, after, before
            )
            for jump, one, two in zip(jumps, after, before):
                held[half - 1 + jump], held[1 - half - jump] = one, two
        columns.append(all_rows(shares[panel], arrived))
        if following:
            shares.append(line_shares(panel + 1, following))
    ends = lax.ppermute(
        jnp.where(chip < half, last[1], last[0]),
        "col",
        [
            (2 * one + which, 2 * two + which)
            for one, two in ((half, 0), (half - 1, chips - 1))
            for which in range(2)
        ],
    )
    return near, held, ends, columns, projected, images


def scatter_step(value, bit):
    half = value.shape[0] // 2
    upper = (lax.axis_index("row") // bit) % 2
    sent = lax.dynamic_slice_in_dim(value, (1 - upper) * half, half, 0)
    kept = lax.dynamic_slice_in_dim(value, upper * half, half, 0)
    return swap_rows(sent, bit), kept


def gather_step(value, bit):
    upper = (lax.axis_index("row") // bit) % 2
    return ordered(upper == 0, value, swap_rows(value, bit), 1)


def line_step(value, hop, chips):
    middle = chips // 2
    place = lax.axis_index("col") // 2
    if hop < middle:
        pairs = [(hop, hop + 1), (chips - 1 - hop, chips - 2 - hop)]
    else:
        hop = chips - 2 - hop
        pairs = [(hop + 1, hop), (chips - 2 - hop, chips - 1 - hop)]
    arrived = lax.ppermute(
        value, "col", [(2 * one + core, 2 * two + core) for one, two in pairs for core in range(2)]
    )

    def combine(value, arrived):
        if pairs[0][0] < pairs[0][1]:
            return value + arrived
        return jnp.where((place == pairs[0][1]) | (place == pairs[1][1]), arrived, value)

    return arrived, combine


def split(value):
    high = lax.reduce_precision(value, 8, 7)
    return high.astype(bf16), (value - high).astype(bf16)


def region(run, *operands):
    results = jax.eval_shape(run, *operands)

    def nothing(*_):
        return jax.tree.map(lambda one: jnp.zeros(one.shape, one.dtype), results)

    return lax.cond(lax.axis_index("col") >= 0, run, nothing, *operands)


def together(*values):
    return lax.optimization_barrier(values)


def body(window, reflectors, factors):
    row_count = lax.axis_size("row")
    chips = lax.axis_size("col") // 2
    row, chip = lax.axis_index("row"), lax.axis_index("col") // 2
    lower = chip < chips // 2
    rows, cols = window.shape
    panels = reflectors.shape[0]
    bits = [1 << bit for bit in range(row_count.bit_length() - 1)]
    orders = [bits[::-1] if panel % 2 else bits for panel in range(panels)]
    slivers = jnp.swapaxes(reflectors, 1, 2)
    near, held, ends, columns, near_projected, images = gather_vectors(
        slivers, row_count, chips, window
    )
    summed = [lax.psum(one, "col") for one in images]
    near_parts = [
        near_projected[near.shape[0] // panels * panel : near.shape[0] // panels * (panel + 1)]
        for panel in range(panels)
    ]
    steps = [scatter_step(one, order[0]) for one, order in zip(near_parts, orders)]
    last_columns, *images = together(columns[-1], *images)
    last_image, ends, *arrived = together(
        image(window, last_columns), ends, *[one for one, _ in steps]
    )
    near_parts = [one + kept for one, (_, kept) in zip(arrived, steps)]
    summed.append(lax.psum(last_image, "col"))
    half = chips // 2
    held[chips - 1], held[1 - chips] = ends, ends
    far = jnp.stack(
        [
            by_chip(lambda one: held[(1 - one // half) * half + place - one])
            for place in range(half)
        ],
        1,
    )
    columns = jnp.concatenate(columns, 0)
    total = columns.shape[0]
    width = total // panels
    part = width // 2

    def projections(window, near, far, columns, factors, *near_parts):
        near_parts = list(near_parts)
        far = both_cores(far, swap_cores(far))
        far_projected = project(far, window)
        for step in range(1, len(bits)):
            steps = [scatter_step(one, order[step]) for one, order in zip(near_parts, orders)]
            arrived = [one for one, _ in steps]
            if step == 1:
                far_projected, *arrived = together(far_projected, *arrived)
            near_parts = [one + kept for one, (_, kept) in zip(arrived, steps)]
        far_projected, near, far = together(far_projected, near, far)
        far_parts = [far_projected[part * panel : part * (panel + 1)] for panel in range(panels)]
        same, mixed, opposite = small(near, near, 1, 1), small(near, far, 1, 1), small(far, far, 1, 1)

        def of(value, one, two):
            return value[part * one : part * (one + 1), part * two : part * (two + 1)]

        inner = [
            ordered(
                lower,
                ordered(lower, of(same, one, two), of(mixed, one, two), 1),
                ordered(lower, of(mixed, two, one).T, of(opposite, one, two), 1),
                0,
            )
            for one in range(panels)
            for two in range(one + 1, panels)
        ]
        for step in range(len(bits)):
            steps = [scatter_step(one, order[step]) for one, order in zip(far_parts, orders)]
            arrived = [one for one, _ in steps]
            if step + 1 == len(bits):
                arrived, inner = together(arrived, inner)
            far_parts = [one + kept for one, (_, kept) in zip(arrived, steps)]

        mine = [ordered(lower, one, two, 0) for one, two in zip(near_parts, far_parts)]
        crossed = small(jnp.concatenate(mine, 0), columns, 1, 1)
        parts = [jnp.stack([one, two]) for one, two in zip(near_parts, far_parts)]
        others = [swap_rows(one, bits[0]) for one in inner]
        other, parts, others = together(
            swap_cores(crossed),
            [gather_step(one, order[-1]) for one, order in zip(parts, orders)],
            others,
        )
        crossed = crossed + other
        inner = [one + two for one, two in zip(inner, others)]
        arrived, combine = line_step(crossed, 0, chips)
        for step in range(len(bits) - 1)[::-1]:
            parts = [gather_step(one, order[step]) for one, order in zip(parts, orders)]
        for bit in bits[1:]:
            inner = [one + swap_rows(one, bit) for one in inner]
        arrived, parts, inner = together(arrived, parts, inner)
        crossed = combine(crossed, arrived)
        projected = jnp.concatenate(parts, 0).reshape(total, cols)

        joined = factors[0]
        for panel in range(1, panels):
            done = panel * width
            products = jnp.concatenate(
                [
                    inner[one * (panels - 1) - one * (one - 1) // 2 + panel - one - 1]
                    for one in range(panel)
                ],
                0,
            )
            between = -small(joined, small(products, factors[panel]))
            joined = jnp.block([[joined, between], [jnp.zeros((width, done), f32), factors[panel]]])
        def chosen(value, panel, other, dim):
            start = panel * width
            one = lax.slice_in_dim(value, start, start + part, axis=dim)
            two = lax.slice_in_dim(value, start + part, start + width, axis=dim)
            return jnp.where(lower == (other == 0), one, two)

        local = jnp.concatenate(
            [chosen(joined, panel, other, 1) for other in range(2) for panel in range(panels)], 1
        )
        both = jnp.concatenate(
            [chosen(local, panel, other, 0) for panel in range(panels) for other in range(2)], 0
        )
        left = split(small(both, projected, 0, 0))
        if chips > 2:
            arrived, combine = line_step(crossed, 1, chips)
            arrived, *left = together(arrived, *left)
            crossed = combine(crossed, arrived)

        def last_step(crossed, window, near, far, *left):
            arrived, combine = line_step(crossed, chips - 2, chips)
            updated, arrived = together(update(window, near, far, *left), arrived)
            return combine(crossed, arrived), updated

        for hop in range(2, chips - 2):
            arrived, combine = line_step(crossed, hop, chips)
            crossed = combine(crossed, arrived)
        if chips > 2:
            crossed, updated = region(last_step, crossed, window, near, far, *left)
        else:
            updated = update(window, near, far, *left)
        everyone = [swap_rows(crossed, distance) for distance in range(1, row_count)]
        right, everyone = together(split(small(joined, columns)), everyone)
        everyone = [crossed] + everyone
        crossed = jnp.zeros((panels, 2, part, total), f32)
        for distance, value in enumerate(everyone):
            source = row ^ distance
            value = value.reshape(panels, 2, -1, total)
            for panel, order in enumerate(orders):
                place, size = 0, part
                for bit in order:
                    size = size // 2
                    place = place + (source // bit) % 2 * size
                crossed = lax.dynamic_update_slice(
                    crossed, value[panel : panel + 1], (panel, 0, place, 0)
                )
        between = split(small(local, crossed.reshape(total, total), 0, 0))
        return updated, far, between, right

    updated, far, between, right = region(
        projections, window, near, far, columns, factors, *near_parts
    )
    return finish(updated, near, far, summed, between, right)


def solution(mesh):
    placed = (P("row", "col"), P(None, "row", "col"), P())
    return jax.shard_map(
        body, mesh=mesh, in_specs=placed, out_specs=P("row", "col"), check_vma=False
    )
```

```python
import functools

import jax
import jax.numpy as jnp
from jax import lax
from jax.experimental import pallas as pl
from jax.experimental.pallas import tpu as pltpu
from jax.sharding import PartitionSpec as P

f32 = jnp.float32
bf16 = jnp.bfloat16
VMEM_BYTES = 50 * 1024 * 1024


def halves(value):
    high = value.astype(bf16)
    return high, (value - high.astype(f32)).astype(bf16)


def dot(one, two, one_dim=1, two_dim=0):
    return lax.dot_general(
        one, two, (((one_dim,), (two_dim,)), ((), ())), preferred_element_type=f32
    )


def small(one, two, one_dim=1, two_dim=0):
    return lax.dot_general(
        one,
        two,
        (((one_dim,), (two_dim,)), ((), ())),
        precision=lax.Precision.HIGH,
        preferred_element_type=f32,
    )


def call(kernel, grid, in_specs, out_specs, out_shape, scratch=(), aliases=None):
    return pl.pallas_call(
        kernel,
        grid=grid,
        in_specs=in_specs,
        out_specs=out_specs,
        out_shape=out_shape,
        scratch_shapes=scratch,
        input_output_aliases=aliases or {},
        compiler_params=pltpu.CompilerParams(vmem_limit_bytes=VMEM_BYTES),
        cost_estimate=pl.CostEstimate(flops=1, bytes_accessed=1, transcendentals=0),
    )


def three_products(one, two, one_dim=1, two_dim=0):
    (high, low), (other_high, other_low) = one, two
    return dot(high, other_high, one_dim, two_dim) + (
        dot(high, other_low, one_dim, two_dim) + dot(low, other_high, one_dim, two_dim)
    )


def project_kernel(pairs, count, *refs):
    vectors_refs, (window_ref, out_ref) = refs[:count], refs[count : count + 2]
    products_refs, both_ref = refs[count + 2 : -1], refs[-1]
    width = out_ref.shape[0]

    @pl.when(pl.program_id(0) == 0)
    def _():
        values = [halves(ref[...]) for ref in vectors_refs]
        both_ref[:width], both_ref[width:] = values[0]
        for (one, two), ref in zip(pairs, products_refs):
            ref[...] = three_products(values[one], values[two], 1, 1)

    high, low = halves(window_ref[...])
    first = dot(both_ref[...], high)
    out_ref[...] = first[:width] + first[width:] + dot(both_ref[:width], low)


def project(vectors, window, pairs, block=256):
    width, rows = vectors[0].shape
    cols = window.shape[1]
    return call(
        functools.partial(project_kernel, pairs, len(vectors)),
        (cols // block,),
        [pl.BlockSpec((width, rows), lambda i: (0, 0))] * len(vectors)
        + [pl.BlockSpec((rows, block), lambda i: (0, i))],
        [pl.BlockSpec((width, block), lambda i: (0, i))]
        + [pl.BlockSpec((width, width), lambda i: (0, 0))] * len(pairs),
        [jax.ShapeDtypeStruct((width, cols), f32)]
        + [jax.ShapeDtypeStruct((width, width), f32)] * len(pairs),
        [pltpu.VMEM((2 * width, rows), bf16)],
    )(*vectors, window)


def image_kernel(window_ref, vectors_ref, out_ref, both_ref):
    width = vectors_ref.shape[0]

    @pl.when(pl.program_id(0) == 0)
    def _():
        high, low = halves(vectors_ref[...])
        both_ref[:width] = high
        both_ref[width:] = low

    high, low = halves(window_ref[...])
    first = dot(high, both_ref[...], 1, 1)
    out_ref[...] = first[:, :width] + first[:, width:] + dot(low, both_ref[:width], 1, 1)


def image(window, vectors, block=512):
    rows, cols = window.shape
    width = vectors.shape[0]
    block = min(block, rows)
    return call(
        image_kernel,
        (rows // block,),
        [
            pl.BlockSpec((block, cols), lambda i: (i, 0)),
            pl.BlockSpec((width, cols), lambda i: (0, 0)),
        ],
        pl.BlockSpec((block, width), lambda i: (i, 0)),
        jax.ShapeDtypeStruct((rows, width), f32),
        [pltpu.VMEM((2 * width, cols), bf16)],
    )(window, vectors)


def cross_kernel(near_ref, far_ref, *refs):
    *image_refs, out_ref = refs

    @pl.when(pl.program_id(0) == 0)
    def _():
        out_ref[...] = jnp.zeros_like(out_ref)

    vectors = jnp.concatenate([near_ref[...], far_ref[...]], 0)
    images = jnp.concatenate([one[...] for one in image_refs], 1)
    out_ref[...] += three_products(halves(vectors), halves(images))


def cross(near, far, images, block=512):
    part, rows = near.shape
    block = min(block, rows)
    width = sum(one.shape[1] for one in images)
    return call(
        cross_kernel,
        (rows // block,),
        [pl.BlockSpec((part, block), lambda i: (0, i))] * 2
        + [pl.BlockSpec((block, one.shape[1]), lambda i: (i, 0)) for one in images],
        pl.BlockSpec((2 * part, width), lambda i: (0, 0)),
        jax.ShapeDtypeStruct((2 * part, width), f32),
    )(near, far, *images)


def prepare_kernel(panels, lower_ref, projected_ref, columns_ref, factors_ref, *refs):
    *inner_refs, local_ref, left_ref, high_ref, low_ref = refs
    lower = lower_ref[0] == 1
    width = factors_ref.shape[1]
    part = width // 2
    joined = factors_ref[0]
    for panel in range(1, panels):
        done = panel * width
        inner = [
            inner_refs[one * (panels - 1) - one * (one - 1) // 2 + panel - one - 1][...]
            for one in range(panel)
        ]
        inner = jnp.concatenate(inner, 0) if panel > 1 else inner[0]
        factor = factors_ref[panel]
        between = three_products(halves(inner), halves(factor))
        between = -three_products(halves(joined), halves(between))
        joined = jnp.concatenate(
            [
                jnp.concatenate([joined, between], 1),
                jnp.concatenate([jnp.zeros((width, done), f32), factor], 1),
            ],
            0,
        )

    def chosen(value, panel, other, dim):
        start = panel * width
        one = lax.slice_in_dim(value, start, start + part, axis=dim)
        two = lax.slice_in_dim(value, start + part, start + width, axis=dim)
        return jnp.where(lower == (other == 0), one, two)

    local = jnp.concatenate(
        [chosen(joined, panel, other, 1) for other in range(2) for panel in range(panels)], 1
    )
    both = jnp.concatenate(
        [chosen(local, panel, other, 0) for panel in range(panels) for other in range(2)], 0
    )
    local_ref[...] = local
    left_ref[...] = three_products(halves(both), halves(projected_ref[...]), 0, 0)
    high_ref[...], low_ref[...] = halves(
        three_products(halves(joined), halves(columns_ref[...]))
    )


def prepare(lower, projected, columns, factors, inner):
    total, cols = projected.shape
    return call(
        functools.partial(prepare_kernel, factors.shape[0]),
        (),
        [pl.BlockSpec(memory_space=pltpu.SMEM)]
        + [pl.BlockSpec(memory_space=pltpu.VMEM)] * (3 + len(inner)),
        [pl.BlockSpec(memory_space=pltpu.VMEM)] * 4,
        [
            jax.ShapeDtypeStruct((total, total), f32),
            jax.ShapeDtypeStruct((total, cols), f32),
            jax.ShapeDtypeStruct((total, cols), bf16),
            jax.ShapeDtypeStruct((total, cols), bf16),
        ],
    )(lower.astype(jnp.int32).reshape(1), projected, columns, factors, *inner)


def finish_kernel(
    window_ref, near_ref, far_ref, local_ref, crossed_ref, left_ref, right_high, right_low, *refs
):
    *image_refs, out_ref, high_ref, low_ref = refs
    width = left_ref.shape[0]

    @pl.when(pl.program_id(0) == 0)
    def _():
        middle = three_products(halves(local_ref[...]), halves(crossed_ref[...]), 0, 0)
        left = left_ref[...] - three_products(halves(middle), (right_high[...], right_low[...]))
        high_ref[:width], low_ref[:width] = halves(left)
        high_ref[width:], low_ref[width:] = right_high[...], right_low[...]

    both = jnp.concatenate(
        [near_ref[...].T, far_ref[...].T] + [one[...] for one in image_refs], 1
    )
    out_ref[...] = window_ref[...] - three_products(halves(both), (high_ref[...], low_ref[...]))


def finish(window, near, far, local, crossed, left, right, images, block=512):
    rows, cols = window.shape
    part, width = near.shape[0], local.shape[0]
    block = min(block, rows)
    return call(
        finish_kernel,
        (rows // block,),
        [
            pl.BlockSpec((block, cols), lambda i: (i, 0)),
            pl.BlockSpec((part, block), lambda i: (0, i)),
            pl.BlockSpec((part, block), lambda i: (0, i)),
        ]
        + [pl.BlockSpec((width, width), lambda i: (0, 0))] * 2
        + [pl.BlockSpec((width, cols), lambda i: (0, 0))] * 3
        + [pl.BlockSpec((block, one.shape[1]), lambda i: (i, 0)) for one in images],
        pl.BlockSpec((block, cols), lambda i: (i, 0)),
        jax.ShapeDtypeStruct((rows, cols), f32),
        [pltpu.VMEM((2 * width, cols), bf16)] * 2,
    )(window, near, far, local, crossed, left, *right, *images)


def swap_cores(value):
    count = lax.axis_size("col")
    return lax.ppermute(value, "col", [(col, col ^ 1) for col in range(count)])


def swap_chips(value, distance):
    count = lax.axis_size("col")
    return lax.ppermute(value, "col", [(col, col ^ (2 * distance)) for col in range(count)])


def swap_rows(value, distance):
    count = lax.axis_size("row")
    return lax.ppermute(value, "row", [(row, row ^ distance) for row in range(count)])


def at(value, index, dim):
    return lax.dynamic_index_in_dim(value, index, dim, keepdims=False)


def put(whole, value, index, dim):
    return lax.dynamic_update_slice_in_dim(whole, jnp.expand_dims(value, dim), index, dim)


def together(*values):
    return lax.optimization_barrier(values)


def region(run, *operands):
    results = jax.eval_shape(run, *operands)

    def nothing(*_):
        return jax.tree.map(lambda one: jnp.zeros(one.shape, one.dtype), results)

    return lax.cond(lax.axis_index("col") >= 0, run, nothing, *operands)


def ordered(condition, one, two, dim):
    return jnp.concatenate([jnp.where(condition, one, two), jnp.where(condition, two, one)], dim)


def by_chip(choose):
    chip = lax.axis_index("col") // 2
    value = choose(0)
    for one in range(1, lax.axis_size("col") // 2):
        value = jnp.where(chip == one, choose(one), value)
    return value


def send_along(value, chips, step, count=None):
    count = chips if count is None else count
    ends = range(count) if step < 0 else range(chips - count, chips)
    return lax.ppermute(
        value,
        "col",
        [
            (2 * (chip - step) + core, 2 * chip + core)
            for chip in ends
            for core in range(2)
            if 0 <= chip - step < chips
        ],
    )


def both_cores(mine, other):
    core = lax.axis_index("col") % 2
    pairs = []
    for place in range(mine.shape[1]):
        one, two = mine[:, place], other[:, place]
        pairs += [jnp.where(core == 0, one, two), jnp.where(core == 0, two, one)]
    return jnp.concatenate(pairs, 1).reshape(-1, mine.shape[-1])


def gather_vectors(slivers, row_count, chips, window):
    col_index, row = lax.axis_index("col"), lax.axis_index("row")
    core, chip = col_index % 2, col_index // 2
    panels, piece, rows = slivers.shape
    cols = rows // 2
    share = 2 * piece // row_count
    distances = range(1, row_count)
    half = chips // 2

    mine = lax.dynamic_slice_in_dim(slivers, core * cols, cols, 2)
    other = swap_cores(lax.dynamic_slice_in_dim(slivers, (1 - core) * cols, cols, 2))
    shares = ordered(core == 0, mine, other, 1).reshape(panels, row_count, share, cols)
    arrived = [swap_rows(at(shares, row ^ distance, 1), distance) for distance in distances]
    held = {0: slivers}
    for step in range(1, half):
        after, before, *arrived = together(
            send_along(held[step - 1], chips, -1), send_along(held[1 - step], chips, 1), *arrived
        )
        held[step], held[-step] = after, before
    by_row = jnp.zeros((panels, row_count, share, cols), f32)
    by_row = put(by_row, at(shares, row, 1), row, 1)
    for distance, value in zip(distances, arrived):
        by_row = put(by_row, value, row ^ distance, 1)

    near = jnp.stack(
        [by_chip(lambda one: held[one // half * half + place - one]) for place in range(half)], 1
    )

    def along_line(panel):
        return [swap_chips(at(by_row[panel], chip ^ distance, 0), distance) for distance in distances]

    def line_shares(panel, arrived):
        shares = jnp.zeros((row_count, share, cols), f32)
        shares = put(shares, at(by_row[panel], chip, 0), chip, 0)
        for distance, value in zip(distances, arrived):
            shares = put(shares, value, chip ^ distance, 0)
        return shares

    def all_rows(shares, arrived):
        whole = jnp.zeros((row_count, row_count, share, cols), f32)
        whole = put(whole, shares, row, 1)
        for distance, value in zip(distances, arrived):
            whole = put(whole, value, row ^ distance, 1)
        return whole.reshape(2 * chips * piece, cols)

    other, arrived = together(swap_cores(near), along_line(0))
    near = both_cores(near, other)
    shares = [line_shares(0, arrived)]
    last = (held[half - 1], held[1 - half])
    *last, near, shares[0] = together(*last, near, shares[0])

    columns, images = [], []
    for panel in range(panels):
        arrived = [swap_rows(shares[panel], distance) for distance in distances]
        following = along_line(panel + 1) if panel + 1 < panels else []
        if panel == 0:
            projected, arrived, following = together(project([near], window, [(0, 0)]), arrived, following)
        else:
            jumps = range(1, half)
            after = [send_along(last[0], chips, -jump, chips - half - jump + 1) for jump in jumps]
            before = [send_along(last[1], chips, jump, chips - half - jump + 1) for jump in jumps]
            images.append(image(window, columns[-1]))
            images[-1], arrived, following, after, before = together(
                images[-1], arrived, following, after, before
            )
            for jump, one, two in zip(jumps, after, before):
                held[half - 1 + jump], held[1 - half - jump] = one, two
        columns.append(all_rows(shares[panel], arrived))
        if following:
            shares.append(line_shares(panel + 1, following))
    ends = lax.ppermute(
        jnp.where(chip < half, last[1], last[0]),
        "col",
        [
            (2 * one + which, 2 * two + which)
            for one, two in ((half, 0), (half - 1, chips - 1))
            for which in range(2)
        ],
    )
    return near, held, ends, columns, projected, images


def scatter_step(value, bit):
    half = value.shape[0] // 2
    upper = (lax.axis_index("row") // bit) % 2
    sent = lax.dynamic_slice_in_dim(value, (1 - upper) * half, half, 0)
    kept = lax.dynamic_slice_in_dim(value, upper * half, half, 0)
    return swap_rows(sent, bit), kept


def gather_step(value, bit):
    upper = (lax.axis_index("row") // bit) % 2
    return ordered(upper == 0, value, swap_rows(value, bit), 1)


def line_step(value, hop, chips):
    middle = chips // 2
    place = lax.axis_index("col") // 2
    if hop < middle:
        pairs = [(hop, hop + 1), (chips - 1 - hop, chips - 2 - hop)]
    else:
        hop = chips - 2 - hop
        pairs = [(hop + 1, hop), (chips - 2 - hop, chips - 1 - hop)]
    arrived = lax.ppermute(
        value, "col", [(2 * one + core, 2 * two + core) for one, two in pairs for core in range(2)]
    )

    def combine(value, arrived):
        if pairs[0][0] < pairs[0][1]:
            return value + arrived
        return jnp.where((place == pairs[0][1]) | (place == pairs[1][1]), arrived, value)

    return arrived, combine


def region(run, *operands):
    results = jax.eval_shape(run, *operands)

    def nothing(*_):
        return jax.tree.map(lambda one: jnp.zeros(one.shape, one.dtype), results)

    return lax.cond(lax.axis_index("col") >= 0, run, nothing, *operands)


def together(*values):
    return lax.optimization_barrier(values)


def body(window, reflectors, factors):
    row_count = lax.axis_size("row")
    chips = lax.axis_size("col") // 2
    row, chip = lax.axis_index("row"), lax.axis_index("col") // 2
    lower = chip < chips // 2
    rows, cols = window.shape
    panels = reflectors.shape[0]
    bits = [1 << bit for bit in range(row_count.bit_length() - 1)]
    orders = [bits[::-1] if panel % 2 else bits for panel in range(panels)]
    slivers = jnp.swapaxes(reflectors, 1, 2)
    near, held, ends, columns, (near_projected, same), images = gather_vectors(
        slivers, row_count, chips, window
    )
    part = near.shape[0] // panels
    width = 2 * part
    total = panels * width
    near_parts = [near_projected[part * panel : part * (panel + 1)] for panel in range(panels)]
    steps = [scatter_step(one, order[0]) for one, order in zip(near_parts, orders)]
    last_columns, *images = together(columns[-1], *images)
    last_image, ends, *arrived = together(
        image(window, last_columns), ends, *[one for one, _ in steps]
    )
    held[chips - 1], held[1 - chips] = ends, ends
    half = chips // 2
    far = jnp.stack(
        [
            by_chip(lambda one: held[(1 - one // half) * half + place - one])
            for place in range(half)
        ],
        1,
    )
    images.append(last_image)
    near_parts = [one + kept for one, (_, kept) in zip(arrived, steps)]
    summed = [lax.psum(one, "col") for one in images]
    columns = jnp.concatenate(columns, 0)

    def factors_of(window, near, far, same, columns, factors, images, near_parts):
        far = both_cores(far, swap_cores(far))
        crossed = cross(near, far, images)
        crossed = ordered(lower, crossed[: total // 2], crossed[total // 2 :], 0)
        sums = [crossed[: total // 2], crossed[total // 2 :]]
        steps = [scatter_step(one, order[0]) for one, order in zip(sums, (bits, bits[::-1]))]
        near_steps = [scatter_step(one, order[1]) for one, order in zip(near_parts, orders)]
        (far_projected, opposite, crossing, mixed), arrived, near_arrived = together(
            project([far, near], window, [(0, 0), (0, 1), (1, 0)]),
            [one for one, _ in steps],
            [one for one, _ in near_steps],
        )
        sums = [one + kept for one, (_, kept) in zip(arrived, steps)]
        near_parts = [one + kept for one, (_, kept) in zip(near_arrived, near_steps)]
        for step in range(2, len(bits)):
            steps = [scatter_step(one, order[step]) for one, order in zip(near_parts, orders)]
            near_parts = [one + kept for one, kept in steps]
        far_parts = [far_projected[part * panel : part * (panel + 1)] for panel in range(panels)]
        for step in range(len(bits)):
            far_steps = [scatter_step(one, order[step]) for one, order in zip(far_parts, orders)]
            steps = []
            if step + 1 < len(bits):
                steps = [
                    scatter_step(one, order[step + 1])
                    for one, order in zip(sums, (bits, bits[::-1]))
                ]
            else:
                crossed = jnp.concatenate(sums, 0)
                steps = [(swap_cores(crossed), crossed)]
            arrived, far_arrived = together([one for one, _ in steps], [one for one, _ in far_steps])
            sums = [one + kept for one, (_, kept) in zip(arrived, steps)]
            far_parts = [one + kept for one, (_, kept) in zip(far_arrived, far_steps)]
        (crossed,) = sums

        def of(value, one, two):
            return value[part * one : part * (one + 1), part * two : part * (two + 1)]

        inner = [
            ordered(
                lower,
                ordered(lower, of(same, one, two), of(mixed, one, two), 1),
                ordered(lower, of(crossing, one, two), of(opposite, one, two), 1),
                0,
            )
            for one in range(panels)
            for two in range(one + 1, panels)
        ]
        parts = [jnp.stack([one, two]) for one, two in zip(near_parts, far_parts)]
        hops = chips - 1
        for step, bit in enumerate(bits):
            others = [swap_rows(one, bit) for one in inner]
            parts = [gather_step(one, order[-1 - step]) for one, order in zip(parts, orders)]
            if step < hops:
                arrived, combine = line_step(crossed, step, chips)
                parts, others, arrived = together(parts, others, arrived)
                crossed = combine(crossed, arrived)
            else:
                parts, others = together(parts, others)
            inner = [one + two for one, two in zip(inner, others)]
        projected = jnp.concatenate(parts, 0).reshape(total, cols)

        for hop in range(len(bits), hops - 1):
            arrived, combine = line_step(crossed, hop, chips)
            crossed = combine(crossed, arrived)
        local, left, *right = prepare(lower, projected, columns, factors, inner)
        if len(bits) < hops:
            arrived, combine = line_step(crossed, hops - 1, chips)
            arrived, local, left, right = together(arrived, local, left, right)
            crossed = combine(crossed, arrived)
        everyone = [crossed] + [swap_rows(crossed, distance) for distance in range(1, row_count)]
        crossed = jnp.zeros((2, total // 2, total), f32)
        for distance, value in enumerate(everyone):
            source = row ^ distance
            for other, order in enumerate((bits, bits[::-1])):
                place, size = 0, total // 2
                for bit in order:
                    size = size // 2
                    place = place + (source // bit) % 2 * size
                crossed = lax.dynamic_update_slice(
                    crossed, value[other * size : (other + 1) * size][None], (other, place, 0)
                )
        crossed = crossed.reshape(2, panels, part, total)
        crossed = jnp.concatenate(
            [crossed[other, panel] for panel in range(panels) for other in range(2)], 0
        )
        return far, local, crossed, left, right

    far, local, crossed, left, right = region(
        factors_of, window, near, far, same, columns, factors, images, near_parts
    )
    return finish(window, near, far, local, crossed, left, right, summed)


def solution(mesh):
    placed = (P("row", "col"), P(None, "row", "col"), P())
    return jax.shard_map(
        body, mesh=mesh, in_specs=placed, out_specs=P("row", "col"), check_vma=False
    )
```

```python
import functools

import jax
import jax.numpy as jnp
from jax import lax
from jax.experimental import pallas as pl
from jax.experimental.pallas import tpu as pltpu
from jax.sharding import PartitionSpec as P

f32 = jnp.float32
bf16 = jnp.bfloat16
MIB = 1024 * 1024


def halves(value):
    high = value.astype(bf16)
    return high, (value - high.astype(f32)).astype(bf16)


def dot(one, two, one_dim=1, two_dim=0):
    return lax.dot_general(
        one, two, (((one_dim,), (two_dim,)), ((), ())), preferred_element_type=f32
    )


def small(one, two, one_dim=1, two_dim=0):
    return lax.dot_general(
        one,
        two,
        (((one_dim,), (two_dim,)), ((), ())),
        precision=lax.Precision.HIGH,
        preferred_element_type=f32,
    )


def call(kernel, mebibytes, grid, in_specs, out_specs, out_shape, scratch=()):
    return pl.pallas_call(
        kernel,
        grid=grid,
        in_specs=in_specs,
        out_specs=out_specs,
        out_shape=out_shape,
        scratch_shapes=scratch,
        compiler_params=pltpu.CompilerParams(vmem_limit_bytes=mebibytes * MIB),
        cost_estimate=pl.CostEstimate(flops=1, bytes_accessed=1, transcendentals=0),
    )


def three_products(one, two, one_dim=1, two_dim=0):
    (high, low), (other_high, other_low) = one, two
    return dot(high, other_high, one_dim, two_dim) + (
        dot(high, other_low, one_dim, two_dim) + dot(low, other_high, one_dim, two_dim)
    )


def project_kernel(pairs, count, *refs):
    vectors_refs, (window_ref, out_ref) = refs[:count], refs[count : count + 2]
    products_refs, both_ref = refs[count + 2 : -1], refs[-1]
    width = out_ref.shape[0]

    @pl.when(pl.program_id(0) == 0)
    def _():
        values = [halves(ref[...]) for ref in vectors_refs]
        both_ref[:width], both_ref[width:] = values[0]
        for (one, two), ref in zip(pairs, products_refs):
            ref[...] = three_products(values[one], values[two], 1, 1)

    high, low = halves(window_ref[...])
    first = dot(both_ref[...], high)
    out_ref[...] = first[:width] + first[width:] + dot(both_ref[:width], low)


def project(vectors, window, pairs, block=256):
    width, rows = vectors[0].shape
    cols = window.shape[1]
    return call(
        functools.partial(project_kernel, pairs, len(vectors)),
        36,
        (cols // block,),
        [pl.BlockSpec((width, rows), lambda i: (0, 0))] * len(vectors)
        + [pl.BlockSpec((rows, block), lambda i: (0, i))],
        [pl.BlockSpec((width, block), lambda i: (0, i))]
        + [pl.BlockSpec((width, width), lambda i: (0, 0))] * len(pairs),
        [jax.ShapeDtypeStruct((width, cols), f32)]
        + [jax.ShapeDtypeStruct((width, width), f32)] * len(pairs),
        [pltpu.VMEM((2 * width, rows), bf16)],
    )(*vectors, window)


def image_kernel(window_ref, vectors_ref, out_ref, both_ref):
    width = vectors_ref.shape[0]

    @pl.when(pl.program_id(0) == 0)
    def _():
        high, low = halves(vectors_ref[...])
        both_ref[:width] = high
        both_ref[width:] = low

    high, low = halves(window_ref[...])
    first = dot(high, both_ref[...], 1, 1)
    out_ref[...] = first[:, :width] + first[:, width:] + dot(low, both_ref[:width], 1, 1)


def image(window, vectors, block=512):
    rows, cols = window.shape
    width = vectors.shape[0]
    block = min(block, rows)
    return call(
        image_kernel,
        22,
        (rows // block,),
        [
            pl.BlockSpec((block, cols), lambda i: (i, 0)),
            pl.BlockSpec((width, cols), lambda i: (0, 0)),
        ],
        pl.BlockSpec((block, width), lambda i: (i, 0)),
        jax.ShapeDtypeStruct((rows, width), f32),
        [pltpu.VMEM((2 * width, cols), bf16)],
    )(window, vectors)


def cross_kernel(near_ref, far_ref, *refs):
    *image_refs, out_ref = refs

    @pl.when(pl.program_id(0) == 0)
    def _():
        out_ref[...] = jnp.zeros_like(out_ref)

    vectors = jnp.concatenate([near_ref[...], far_ref[...]], 0)
    images = jnp.concatenate([one[...] for one in image_refs], 1)
    out_ref[...] += three_products(halves(vectors), halves(images))


def cross(near, far, images, block=512):
    part, rows = near.shape
    block = min(block, rows)
    width = sum(one.shape[1] for one in images)
    return call(
        cross_kernel,
        16,
        (rows // block,),
        [pl.BlockSpec((part, block), lambda i: (0, i))] * 2
        + [pl.BlockSpec((block, one.shape[1]), lambda i: (i, 0)) for one in images],
        pl.BlockSpec((2 * part, width), lambda i: (0, 0)),
        jax.ShapeDtypeStruct((2 * part, width), f32),
    )(near, far, *images)


def prepare_kernel(panels, lower_ref, projected_ref, columns_ref, factors_ref, *refs):
    *inner_refs, local_ref, left_ref, high_ref, low_ref = refs
    lower = lower_ref[0] == 1
    width = factors_ref.shape[1]
    part = width // 2
    joined = factors_ref[0]
    for panel in range(1, panels):
        done = panel * width
        inner = [
            inner_refs[one * (panels - 1) - one * (one - 1) // 2 + panel - one - 1][...]
            for one in range(panel)
        ]
        inner = jnp.concatenate(inner, 0) if panel > 1 else inner[0]
        factor = factors_ref[panel]
        between = three_products(halves(inner), halves(factor))
        between = -three_products(halves(joined), halves(between))
        joined = jnp.concatenate(
            [
                jnp.concatenate([joined, between], 1),
                jnp.concatenate([jnp.zeros((width, done), f32), factor], 1),
            ],
            0,
        )

    def chosen(value, panel, other, dim):
        start = panel * width
        one = lax.slice_in_dim(value, start, start + part, axis=dim)
        two = lax.slice_in_dim(value, start + part, start + width, axis=dim)
        return jnp.where(lower == (other == 0), one, two)

    local = jnp.concatenate(
        [chosen(joined, panel, other, 1) for other in range(2) for panel in range(panels)], 1
    )
    both = jnp.concatenate(
        [chosen(local, panel, other, 0) for panel in range(panels) for other in range(2)], 0
    )
    local_ref[...] = local
    left_ref[...] = three_products(halves(both), halves(projected_ref[...]), 0, 0)
    high_ref[...], low_ref[...] = halves(
        three_products(halves(joined), halves(columns_ref[...]))
    )


def prepare(lower, projected, columns, factors, inner):
    total, cols = projected.shape
    return call(
        functools.partial(prepare_kernel, factors.shape[0]),
        36,
        (),
        [pl.BlockSpec(memory_space=pltpu.SMEM)]
        + [pl.BlockSpec(memory_space=pltpu.VMEM)] * (3 + len(inner)),
        [pl.BlockSpec(memory_space=pltpu.VMEM)] * 4,
        [
            jax.ShapeDtypeStruct((total, total), f32),
            jax.ShapeDtypeStruct((total, cols), f32),
            jax.ShapeDtypeStruct((total, cols), bf16),
            jax.ShapeDtypeStruct((total, cols), bf16),
        ],
    )(lower.astype(jnp.int32).reshape(1), projected, columns, factors, *inner)


def finish_kernel(
    window_ref, near_ref, far_ref, local_ref, crossed_ref, left_ref, right_high, right_low, *refs
):
    *image_refs, out_ref, high_ref, low_ref = refs
    width = left_ref.shape[0]

    @pl.when(pl.program_id(0) == 0)
    def _():
        middle = three_products(halves(local_ref[...]), halves(crossed_ref[...]), 0, 0)
        left = left_ref[...] - three_products(halves(middle), (right_high[...], right_low[...]))
        high_ref[:width], low_ref[:width] = halves(left)
        high_ref[width:], low_ref[width:] = right_high[...], right_low[...]

    both = jnp.concatenate(
        [near_ref[...].T, far_ref[...].T] + [one[...] for one in image_refs], 1
    )
    out_ref[...] = window_ref[...] - three_products(halves(both), (high_ref[...], low_ref[...]))


def finish(window, near, far, local, crossed, left, right, images, block=512):
    rows, cols = window.shape
    part, width = near.shape[0], local.shape[0]
    block = min(block, rows)
    return call(
        finish_kernel,
        52,
        (rows // block,),
        [
            pl.BlockSpec((block, cols), lambda i: (i, 0)),
            pl.BlockSpec((part, block), lambda i: (0, i)),
            pl.BlockSpec((part, block), lambda i: (0, i)),
        ]
        + [pl.BlockSpec((width, width), lambda i: (0, 0))] * 2
        + [pl.BlockSpec((width, cols), lambda i: (0, 0))] * 3
        + [pl.BlockSpec((block, one.shape[1]), lambda i: (i, 0)) for one in images],
        pl.BlockSpec((block, cols), lambda i: (i, 0)),
        jax.ShapeDtypeStruct((rows, cols), f32),
        [pltpu.VMEM((2 * width, cols), bf16)] * 2,
    )(window, near, far, local, crossed, left, *right, *images)


def swap_cores(value):
    count = lax.axis_size("col")
    return lax.ppermute(value, "col", [(col, col ^ 1) for col in range(count)])


def swap_chips(value, distance):
    count = lax.axis_size("col")
    return lax.ppermute(value, "col", [(col, col ^ (2 * distance)) for col in range(count)])


def swap_rows(value, distance):
    count = lax.axis_size("row")
    return lax.ppermute(value, "row", [(row, row ^ distance) for row in range(count)])


def at(value, index, dim):
    return lax.dynamic_index_in_dim(value, index, dim, keepdims=False)


def put(whole, value, index, dim):
    return lax.dynamic_update_slice_in_dim(whole, jnp.expand_dims(value, dim), index, dim)


def together(*values):
    return lax.optimization_barrier(values)


def region(run, *operands):
    results = jax.eval_shape(run, *operands)

    def nothing(*_):
        return jax.tree.map(lambda one: jnp.zeros(one.shape, one.dtype), results)

    return lax.cond(lax.axis_index("col") >= 0, run, nothing, *operands)


def ordered(condition, one, two, dim):
    return jnp.concatenate([jnp.where(condition, one, two), jnp.where(condition, two, one)], dim)


def by_chip(choose):
    chip = lax.axis_index("col") // 2
    value = choose(0)
    for one in range(1, lax.axis_size("col") // 2):
        value = jnp.where(chip == one, choose(one), value)
    return value


def send_along(value, chips, step, count=None):
    count = chips if count is None else count
    ends = range(count) if step < 0 else range(chips - count, chips)
    return lax.ppermute(
        value,
        "col",
        [
            (2 * (chip - step) + core, 2 * chip + core)
            for chip in ends
            for core in range(2)
            if 0 <= chip - step < chips
        ],
    )


def both_cores(mine, other):
    core = lax.axis_index("col") % 2
    pairs = []
    for place in range(mine.shape[1]):
        one, two = mine[:, place], other[:, place]
        pairs += [jnp.where(core == 0, one, two), jnp.where(core == 0, two, one)]
    return jnp.concatenate(pairs, 1).reshape(-1, mine.shape[-1])


def gather_vectors(slivers, row_count, chips, window):
    col_index, row = lax.axis_index("col"), lax.axis_index("row")
    core, chip = col_index % 2, col_index // 2
    panels, piece, rows = slivers.shape
    cols = rows // 2
    share = 2 * piece // row_count
    distances = range(1, row_count)
    half = chips // 2

    mine = lax.dynamic_slice_in_dim(slivers, core * cols, cols, 2)
    other = swap_cores(lax.dynamic_slice_in_dim(slivers, (1 - core) * cols, cols, 2))
    shares = ordered(core == 0, mine, other, 1).reshape(panels, row_count, share, cols)
    arrived = [swap_rows(at(shares, row ^ distance, 1), distance) for distance in distances]
    held = {0: slivers}
    for step in range(1, half):
        after, before, *arrived = together(
            send_along(held[step - 1], chips, -1), send_along(held[1 - step], chips, 1), *arrived
        )
        held[step], held[-step] = after, before
    by_row = jnp.zeros((panels, row_count, share, cols), f32)
    by_row = put(by_row, at(shares, row, 1), row, 1)
    for distance, value in zip(distances, arrived):
        by_row = put(by_row, value, row ^ distance, 1)

    near = jnp.stack(
        [by_chip(lambda one: held[one // half * half + place - one]) for place in range(half)], 1
    )

    def along_line(panel):
        return [swap_chips(at(by_row[panel], chip ^ distance, 0), distance) for distance in distances]

    def line_shares(panel, arrived):
        shares = jnp.zeros((row_count, share, cols), f32)
        shares = put(shares, at(by_row[panel], chip, 0), chip, 0)
        for distance, value in zip(distances, arrived):
            shares = put(shares, value, chip ^ distance, 0)
        return shares

    def all_rows(shares, arrived):
        whole = jnp.zeros((row_count, row_count, share, cols), f32)
        whole = put(whole, shares, row, 1)
        for distance, value in zip(distances, arrived):
            whole = put(whole, value, row ^ distance, 1)
        return whole.reshape(2 * chips * piece, cols)

    other, arrived = together(swap_cores(near), along_line(0))
    near = both_cores(near, other)
    shares = [line_shares(0, arrived)]
    last = (held[half - 1], held[1 - half])
    *last, near, shares[0] = together(*last, near, shares[0])

    columns, images = [], []
    for panel in range(panels):
        arrived = [swap_rows(shares[panel], distance) for distance in distances]
        following = along_line(panel + 1) if panel + 1 < panels else []
        if panel == 0:
            projected, arrived, following = together(project([near], window, [(0, 0)]), arrived, following)
        else:
            jumps = range(1, half)
            after = [send_along(last[0], chips, -jump, chips - half - jump + 1) for jump in jumps]
            before = [send_along(last[1], chips, jump, chips - half - jump + 1) for jump in jumps]
            images.append(image(window, columns[-1]))
            images[-1], arrived, following, after, before = together(
                images[-1], arrived, following, after, before
            )
            for jump, one, two in zip(jumps, after, before):
                held[half - 1 + jump], held[1 - half - jump] = one, two
        columns.append(all_rows(shares[panel], arrived))
        if following:
            shares.append(line_shares(panel + 1, following))
    ends = lax.ppermute(
        jnp.where(chip < half, last[1], last[0]),
        "col",
        [
            (2 * one + which, 2 * two + which)
            for one, two in ((half, 0), (half - 1, chips - 1))
            for which in range(2)
        ],
    )
    return near, held, ends, columns, projected, images


def scatter_step(value, bit):
    half = value.shape[0] // 2
    upper = (lax.axis_index("row") // bit) % 2
    sent = lax.dynamic_slice_in_dim(value, (1 - upper) * half, half, 0)
    kept = lax.dynamic_slice_in_dim(value, upper * half, half, 0)
    return swap_rows(sent, bit), kept


def gather_step(value, bit):
    upper = (lax.axis_index("row") // bit) % 2
    return ordered(upper == 0, value, swap_rows(value, bit), 1)


def line_step(value, hop, chips):
    middle = chips // 2
    place = lax.axis_index("col") // 2
    if hop < middle:
        pairs = [(hop, hop + 1), (chips - 1 - hop, chips - 2 - hop)]
    else:
        hop = chips - 2 - hop
        pairs = [(hop + 1, hop), (chips - 2 - hop, chips - 1 - hop)]
    arrived = lax.ppermute(
        value, "col", [(2 * one + core, 2 * two + core) for one, two in pairs for core in range(2)]
    )

    def combine(value, arrived):
        if pairs[0][0] < pairs[0][1]:
            return value + arrived
        return jnp.where((place == pairs[0][1]) | (place == pairs[1][1]), arrived, value)

    return arrived, combine


def region(run, *operands):
    results = jax.eval_shape(run, *operands)

    def nothing(*_):
        return jax.tree.map(lambda one: jnp.zeros(one.shape, one.dtype), results)

    return lax.cond(lax.axis_index("col") >= 0, run, nothing, *operands)


def together(*values):
    return lax.optimization_barrier(values)


def body(window, reflectors, factors):
    row_count = lax.axis_size("row")
    chips = lax.axis_size("col") // 2
    row, chip = lax.axis_index("row"), lax.axis_index("col") // 2
    lower = chip < chips // 2
    rows, cols = window.shape
    panels = reflectors.shape[0]
    bits = [1 << bit for bit in range(row_count.bit_length() - 1)]
    orders = [bits[::-1] if panel % 2 else bits for panel in range(panels)]
    slivers = jnp.swapaxes(reflectors, 1, 2)
    near, held, ends, columns, (near_projected, same), images = gather_vectors(
        slivers, row_count, chips, window
    )
    part = near.shape[0] // panels
    width = 2 * part
    total = panels * width
    near_parts = [near_projected[part * panel : part * (panel + 1)] for panel in range(panels)]
    steps = [scatter_step(one, order[0]) for one, order in zip(near_parts, orders)]
    last_columns, *images = together(columns[-1], *images)
    last_image, ends, *arrived = together(
        image(window, last_columns), ends, *[one for one, _ in steps]
    )
    held[chips - 1], held[1 - chips] = ends, ends
    half = chips // 2
    far = jnp.stack(
        [
            by_chip(lambda one: held[(1 - one // half) * half + place - one])
            for place in range(half)
        ],
        1,
    )
    images.append(last_image)
    near_parts = [one + kept for one, (_, kept) in zip(arrived, steps)]
    summed = [lax.psum(one, "col") for one in images]
    columns = jnp.concatenate(columns, 0)

    def factors_of(window, near, far, same, columns, factors, images, near_parts):
        far = both_cores(far, swap_cores(far))
        crossed = cross(near, far, images)
        crossed = ordered(lower, crossed[: total // 2], crossed[total // 2 :], 0)
        sums = [crossed[: total // 2], crossed[total // 2 :]]
        steps = [scatter_step(one, order[0]) for one, order in zip(sums, (bits, bits[::-1]))]
        near_steps = [scatter_step(one, order[1]) for one, order in zip(near_parts, orders)]
        (far_projected, opposite, crossing, mixed), arrived, near_arrived = together(
            project([far, near], window, [(0, 0), (0, 1), (1, 0)]),
            [one for one, _ in steps],
            [one for one, _ in near_steps],
        )
        sums = [one + kept for one, (_, kept) in zip(arrived, steps)]
        near_parts = [one + kept for one, (_, kept) in zip(near_arrived, near_steps)]
        for step in range(2, len(bits)):
            steps = [scatter_step(one, order[step]) for one, order in zip(near_parts, orders)]
            near_parts = [one + kept for one, kept in steps]
        far_parts = [far_projected[part * panel : part * (panel + 1)] for panel in range(panels)]
        for step in range(len(bits)):
            far_steps = [scatter_step(one, order[step]) for one, order in zip(far_parts, orders)]
            steps = []
            if step + 1 < len(bits):
                steps = [
                    scatter_step(one, order[step + 1])
                    for one, order in zip(sums, (bits, bits[::-1]))
                ]
            else:
                crossed = jnp.concatenate(sums, 0)
                steps = [(swap_cores(crossed), crossed)]
            arrived, far_arrived = together([one for one, _ in steps], [one for one, _ in far_steps])
            sums = [one + kept for one, (_, kept) in zip(arrived, steps)]
            far_parts = [one + kept for one, (_, kept) in zip(far_arrived, far_steps)]
        (crossed,) = sums

        def of(value, one, two):
            return value[part * one : part * (one + 1), part * two : part * (two + 1)]

        inner = [
            ordered(
                lower,
                ordered(lower, of(same, one, two), of(mixed, one, two), 1),
                ordered(lower, of(crossing, one, two), of(opposite, one, two), 1),
                0,
            )
            for one in range(panels)
            for two in range(one + 1, panels)
        ]
        parts = [jnp.stack([one, two]) for one, two in zip(near_parts, far_parts)]
        hops = chips - 1
        for step, bit in enumerate(bits):
            others = [swap_rows(one, bit) for one in inner]
            parts = [gather_step(one, order[-1 - step]) for one, order in zip(parts, orders)]
            if step < hops:
                arrived, combine = line_step(crossed, step, chips)
                parts, others, arrived = together(parts, others, arrived)
                crossed = combine(crossed, arrived)
            else:
                parts, others = together(parts, others)
            inner = [one + two for one, two in zip(inner, others)]
        projected = jnp.concatenate(parts, 0).reshape(total, cols)

        for hop in range(len(bits), hops - 1):
            arrived, combine = line_step(crossed, hop, chips)
            crossed = combine(crossed, arrived)
        local, left, *right = prepare(lower, projected, columns, factors, inner)
        if len(bits) < hops:
            arrived, combine = line_step(crossed, hops - 1, chips)
            arrived, local, left, right = together(arrived, local, left, right)
            crossed = combine(crossed, arrived)
        everyone = [crossed] + [swap_rows(crossed, distance) for distance in range(1, row_count)]
        crossed = jnp.zeros((2, total // 2, total), f32)
        for distance, value in enumerate(everyone):
            source = row ^ distance
            for other, order in enumerate((bits, bits[::-1])):
                place, size = 0, total // 2
                for bit in order:
                    size = size // 2
                    place = place + (source // bit) % 2 * size
                crossed = lax.dynamic_update_slice(
                    crossed, value[other * size : (other + 1) * size][None], (other, place, 0)
                )
        crossed = crossed.reshape(2, panels, part, total)
        crossed = jnp.concatenate(
            [crossed[other, panel] for panel in range(panels) for other in range(2)], 0
        )
        return far, local, crossed, left, right

    far, local, crossed, left, right = region(
        factors_of, window, near, far, same, columns, factors, images, near_parts
    )
    return finish(window, near, far, local, crossed, left, right, summed)


def solution(mesh):
    placed = (P("row", "col"), P(None, "row", "col"), P())
    return jax.shard_map(
        body, mesh=mesh, in_specs=placed, out_specs=P("row", "col"), check_vma=False
    )
```

```python
import functools

import jax
import jax.numpy as jnp
from jax import lax
from jax.experimental import pallas as pl
from jax.experimental.pallas import tpu as pltpu
from jax.sharding import PartitionSpec as P

f32 = jnp.float32
bf16 = jnp.bfloat16
MIB = 1024 * 1024


def halves(value):
    high = value.astype(bf16)
    return high, (value - high.astype(f32)).astype(bf16)


def dot(one, two, one_dim=1, two_dim=0):
    return lax.dot_general(
        one, two, (((one_dim,), (two_dim,)), ((), ())), preferred_element_type=f32
    )


def small(one, two, one_dim=1, two_dim=0):
    return lax.dot_general(
        one,
        two,
        (((one_dim,), (two_dim,)), ((), ())),
        precision=lax.Precision.HIGH,
        preferred_element_type=f32,
    )


def call(kernel, mebibytes, grid, in_specs, out_specs, out_shape, scratch=()):
    return pl.pallas_call(
        kernel,
        grid=grid,
        in_specs=in_specs,
        out_specs=out_specs,
        out_shape=out_shape,
        scratch_shapes=scratch,
        compiler_params=pltpu.CompilerParams(vmem_limit_bytes=mebibytes * MIB),
        cost_estimate=pl.CostEstimate(flops=1, bytes_accessed=1, transcendentals=0),
    )


def three_products(one, two, one_dim=1, two_dim=0):
    (high, low), (other_high, other_low) = one, two
    return dot(high, other_high, one_dim, two_dim) + (
        dot(high, other_low, one_dim, two_dim) + dot(low, other_high, one_dim, two_dim)
    )


def project_kernel(pairs, count, *refs):
    vectors_refs, (window_ref, out_ref) = refs[:count], refs[count : count + 2]
    products_refs, both_ref = refs[count + 2 : -1], refs[-1]
    width = out_ref.shape[0]

    @pl.when(pl.program_id(0) == 0)
    def _():
        values = [halves(ref[...]) for ref in vectors_refs]
        both_ref[:width], both_ref[width:] = values[0]
        for (one, two), ref in zip(pairs, products_refs):
            ref[...] = three_products(values[one], values[two], 1, 1)

    high, low = halves(window_ref[...])
    first = dot(both_ref[...], high)
    out_ref[...] = first[:width] + first[width:] + dot(both_ref[:width], low)


def project(vectors, window, pairs, block=256):
    width, rows = vectors[0].shape
    cols = window.shape[1]
    return call(
        functools.partial(project_kernel, pairs, len(vectors)),
        36,
        (cols // block,),
        [pl.BlockSpec((width, rows), lambda i: (0, 0))] * len(vectors)
        + [pl.BlockSpec((rows, block), lambda i: (0, i))],
        [pl.BlockSpec((width, block), lambda i: (0, i))]
        + [pl.BlockSpec((width, width), lambda i: (0, 0))] * len(pairs),
        [jax.ShapeDtypeStruct((width, cols), f32)]
        + [jax.ShapeDtypeStruct((width, width), f32)] * len(pairs),
        [pltpu.VMEM((2 * width, rows), bf16)],
    )(*vectors, window)


def image_kernel(window_ref, vectors_ref, out_ref, both_ref):
    width = vectors_ref.shape[0]

    @pl.when(pl.program_id(0) == 0)
    def _():
        high, low = halves(vectors_ref[...])
        both_ref[:width] = high
        both_ref[width:] = low

    high, low = halves(window_ref[...])
    first = dot(high, both_ref[...], 1, 1)
    out_ref[...] = first[:, :width] + first[:, width:] + dot(low, both_ref[:width], 1, 1)


def image(window, vectors, block=512):
    rows, cols = window.shape
    width = vectors.shape[0]
    block = min(block, rows)
    return call(
        image_kernel,
        22,
        (rows // block,),
        [
            pl.BlockSpec((block, cols), lambda i: (i, 0)),
            pl.BlockSpec((width, cols), lambda i: (0, 0)),
        ],
        pl.BlockSpec((block, width), lambda i: (i, 0)),
        jax.ShapeDtypeStruct((rows, width), f32),
        [pltpu.VMEM((2 * width, cols), bf16)],
    )(window, vectors)


def cross_kernel(near_ref, far_ref, *refs):
    *image_refs, out_ref = refs

    @pl.when(pl.program_id(0) == 0)
    def _():
        out_ref[...] = jnp.zeros_like(out_ref)

    vectors = jnp.concatenate([near_ref[...], far_ref[...]], 0)
    images = jnp.concatenate([one[...] for one in image_refs], 1)
    out_ref[...] += three_products(halves(vectors), halves(images))


def cross(near, far, images, block=512):
    part, rows = near.shape
    block = min(block, rows)
    width = sum(one.shape[1] for one in images)
    return call(
        cross_kernel,
        16,
        (rows // block,),
        [pl.BlockSpec((part, block), lambda i: (0, i))] * 2
        + [pl.BlockSpec((block, one.shape[1]), lambda i: (i, 0)) for one in images],
        pl.BlockSpec((2 * part, width), lambda i: (0, 0)),
        jax.ShapeDtypeStruct((2 * part, width), f32),
    )(near, far, *images)


def prepare_kernel(panels, lower_ref, projected_ref, columns_ref, factors_ref, *refs):
    *inner_refs, local_ref, left_ref, high_ref, low_ref = refs
    lower = lower_ref[0] == 1
    width = factors_ref.shape[1]
    part = width // 2
    joined = factors_ref[0]
    for panel in range(1, panels):
        done = panel * width
        inner = [
            inner_refs[one * (panels - 1) - one * (one - 1) // 2 + panel - one - 1][...]
            for one in range(panel)
        ]
        inner = jnp.concatenate(inner, 0) if panel > 1 else inner[0]
        factor = factors_ref[panel]
        between = three_products(halves(inner), halves(factor))
        between = -three_products(halves(joined), halves(between))
        joined = jnp.concatenate(
            [
                jnp.concatenate([joined, between], 1),
                jnp.concatenate([jnp.zeros((width, done), f32), factor], 1),
            ],
            0,
        )

    def chosen(value, panel, other, dim):
        start = panel * width
        one = lax.slice_in_dim(value, start, start + part, axis=dim)
        two = lax.slice_in_dim(value, start + part, start + width, axis=dim)
        return jnp.where(lower == (other == 0), one, two)

    local = jnp.concatenate(
        [chosen(joined, panel, other, 1) for other in range(2) for panel in range(panels)], 1
    )
    both = jnp.concatenate(
        [chosen(local, panel, other, 0) for panel in range(panels) for other in range(2)], 0
    )
    local_ref[...] = local
    left_ref[...] = three_products(halves(both), halves(projected_ref[...]), 0, 0)
    high_ref[...], low_ref[...] = halves(
        three_products(halves(joined), halves(columns_ref[...]))
    )


def prepare(lower, projected, columns, factors, inner):
    total, cols = projected.shape
    return call(
        functools.partial(prepare_kernel, factors.shape[0]),
        36,
        (),
        [pl.BlockSpec(memory_space=pltpu.SMEM)]
        + [pl.BlockSpec(memory_space=pltpu.VMEM)] * (3 + len(inner)),
        [pl.BlockSpec(memory_space=pltpu.VMEM)] * 4,
        [
            jax.ShapeDtypeStruct((total, total), f32),
            jax.ShapeDtypeStruct((total, cols), f32),
            jax.ShapeDtypeStruct((total, cols), bf16),
            jax.ShapeDtypeStruct((total, cols), bf16),
        ],
    )(lower.astype(jnp.int32).reshape(1), projected, columns, factors, *inner)


def weights_kernel(
    local_ref, crossed_ref, left_ref, right_high, right_low, high_ref, low_ref
):
    width = left_ref.shape[0]
    middle = three_products(halves(local_ref[...]), halves(crossed_ref[...]), 0, 0)
    left = left_ref[...] - three_products(halves(middle), (right_high[...], right_low[...]))
    high_ref[:width], low_ref[:width] = halves(left)
    high_ref[width:], low_ref[width:] = right_high[...], right_low[...]


def weights(local, crossed, left, right):
    width, cols = left.shape
    return call(
        weights_kernel,
        30,
        (),
        [pl.BlockSpec(memory_space=pltpu.VMEM)] * 5,
        [pl.BlockSpec(memory_space=pltpu.VMEM)] * 2,
        [jax.ShapeDtypeStruct((2 * width, cols), bf16)] * 2,
    )(local, crossed, left, *right)


def finish_kernel(window_ref, near_ref, far_ref, high_ref, low_ref, *refs):
    *image_refs, out_ref = refs
    both = jnp.concatenate(
        [near_ref[...].T, far_ref[...].T] + [one[...] for one in image_refs], 1
    )
    out_ref[...] = window_ref[...] - three_products(halves(both), (high_ref[...], low_ref[...]))


def finish(window, near, far, high, low, images, block=512):
    rows, cols = window.shape
    part, width = near.shape[0], high.shape[0]
    block = min(block, rows)
    return call(
        finish_kernel,
        52,
        (rows // block,),
        [
            pl.BlockSpec((block, cols), lambda i: (i, 0)),
            pl.BlockSpec((part, block), lambda i: (0, i)),
            pl.BlockSpec((part, block), lambda i: (0, i)),
        ]
        + [pl.BlockSpec((width, cols), lambda i: (0, 0))] * 2
        + [pl.BlockSpec((block, one.shape[1]), lambda i: (i, 0)) for one in images],
        pl.BlockSpec((block, cols), lambda i: (i, 0)),
        jax.ShapeDtypeStruct((rows, cols), f32),
    )(window, near, far, high, low, *images)


def swap_cores(value):
    count = lax.axis_size("col")
    return lax.ppermute(value, "col", [(col, col ^ 1) for col in range(count)])


def swap_chips(value, distance):
    count = lax.axis_size("col")
    return lax.ppermute(value, "col", [(col, col ^ (2 * distance)) for col in range(count)])


def swap_rows(value, distance):
    count = lax.axis_size("row")
    return lax.ppermute(value, "row", [(row, row ^ distance) for row in range(count)])


def at(value, index, dim):
    return lax.dynamic_index_in_dim(value, index, dim, keepdims=False)


def put(whole, value, index, dim):
    return lax.dynamic_update_slice_in_dim(whole, jnp.expand_dims(value, dim), index, dim)


def together(*values):
    return lax.optimization_barrier(values)


def region(run, *operands):
    results = jax.eval_shape(run, *operands)

    def nothing(*_):
        return jax.tree.map(lambda one: jnp.zeros(one.shape, one.dtype), results)

    return lax.cond(lax.axis_index("col") >= 0, run, nothing, *operands)


def ordered(condition, one, two, dim):
    return jnp.concatenate([jnp.where(condition, one, two), jnp.where(condition, two, one)], dim)


def by_chip(choose):
    chip = lax.axis_index("col") // 2
    value = choose(0)
    for one in range(1, lax.axis_size("col") // 2):
        value = jnp.where(chip == one, choose(one), value)
    return value


def send_along(value, chips, step, count=None):
    count = chips if count is None else count
    ends = range(count) if step < 0 else range(chips - count, chips)
    return lax.ppermute(
        value,
        "col",
        [
            (2 * (chip - step) + core, 2 * chip + core)
            for chip in ends
            for core in range(2)
            if 0 <= chip - step < chips
        ],
    )


def both_cores(mine, other):
    core = lax.axis_index("col") % 2
    pairs = []
    for one, two in zip(mine, other):
        pairs += [jnp.where(core == 0, one, two), jnp.where(core == 0, two, one)]
    return jnp.concatenate(pairs, 1).reshape(-1, mine[0].shape[-1])


def gather_vectors(slivers, row_count, chips, window):
    col_index, row = lax.axis_index("col"), lax.axis_index("row")
    core, chip = col_index % 2, col_index // 2
    panels, piece, rows = slivers.shape
    cols = rows // 2
    share = 2 * piece // row_count
    distances = range(1, row_count)
    half = chips // 2

    mine = lax.dynamic_slice_in_dim(slivers, core * cols, cols, 2)
    other = swap_cores(lax.dynamic_slice_in_dim(slivers, (1 - core) * cols, cols, 2))
    shares = ordered(core == 0, mine, other, 1).reshape(panels, row_count, share, cols)
    arrived = [swap_rows(at(shares, row ^ distance, 1), distance) for distance in distances]
    held = {0: slivers}
    for step in range(1, half):
        after, before, *arrived = together(
            send_along(held[step - 1], chips, -1), send_along(held[1 - step], chips, 1), *arrived
        )
        held[step], held[-step] = after, before
    by_row = jnp.zeros((panels, row_count, share, cols), f32)
    by_row = put(by_row, at(shares, row, 1), row, 1)
    for distance, value in zip(distances, arrived):
        by_row = put(by_row, value, row ^ distance, 1)

    near = jnp.stack(
        [by_chip(lambda one: held[one // half * half + place - one]) for place in range(half)], 1
    )

    def along_line(panel):
        return [swap_chips(at(by_row[panel], chip ^ distance, 0), distance) for distance in distances]

    def line_shares(panel, arrived):
        shares = jnp.zeros((row_count, share, cols), f32)
        shares = put(shares, at(by_row[panel], chip, 0), chip, 0)
        for distance, value in zip(distances, arrived):
            shares = put(shares, value, chip ^ distance, 0)
        return shares

    def all_rows(shares, arrived):
        whole = jnp.zeros((row_count, row_count, share, cols), f32)
        whole = put(whole, shares, row, 1)
        for distance, value in zip(distances, arrived):
            whole = put(whole, value, row ^ distance, 1)
        return whole.reshape(2 * chips * piece, cols)

    other, arrived = together(swap_cores(near), along_line(0))
    near, other = (
        [value[:, place] for place in range(half)] for value in (near, other)
    )
    near = both_cores(near, other)
    shares = [line_shares(0, arrived)]
    last = (held[half - 1], held[1 - half])
    *last, near, shares[0] = together(*last, near, shares[0])

    columns, images = [], []
    for panel in range(panels):
        arrived = [swap_rows(shares[panel], distance) for distance in distances]
        following = along_line(panel + 1) if panel + 1 < panels else []
        if panel == 0:
            projected, arrived, following = together(project([near], window, [(0, 0)]), arrived, following)
        else:
            jumps = range(1, half)
            after = [send_along(last[0], chips, -jump, chips - half - jump + 1) for jump in jumps]
            before = [send_along(last[1], chips, jump, chips - half - jump + 1) for jump in jumps]
            images.append(image(window, columns[-1]))
            images[-1], arrived, following, after, before = together(
                images[-1], arrived, following, after, before
            )
            for jump, one, two in zip(jumps, after, before):
                held[half - 1 + jump], held[1 - half - jump] = one, two
        columns.append(all_rows(shares[panel], arrived))
        if following:
            shares.append(line_shares(panel + 1, following))
    ends = lax.ppermute(
        jnp.where(chip < half, last[1], last[0]),
        "col",
        [
            (2 * one + which, 2 * two + which)
            for one, two in ((half, 0), (half - 1, chips - 1))
            for which in range(2)
        ],
    )
    return near, held, ends, columns, projected, images


def scatter_step(value, bit):
    half = value.shape[0] // 2
    upper = (lax.axis_index("row") // bit) % 2
    sent = lax.dynamic_slice_in_dim(value, (1 - upper) * half, half, 0)
    kept = lax.dynamic_slice_in_dim(value, upper * half, half, 0)
    return swap_rows(sent, bit), kept


def gather_step(value, bit):
    upper = (lax.axis_index("row") // bit) % 2
    return ordered(upper == 0, value, swap_rows(value, bit), 1)


def line_step(value, hop, chips):
    middle = chips // 2
    place = lax.axis_index("col") // 2
    if hop < middle:
        pairs = [(hop, hop + 1), (chips - 1 - hop, chips - 2 - hop)]
    else:
        hop = chips - 2 - hop
        pairs = [(hop + 1, hop), (chips - 2 - hop, chips - 1 - hop)]
    arrived = lax.ppermute(
        value, "col", [(2 * one + core, 2 * two + core) for one, two in pairs for core in range(2)]
    )

    def combine(value, arrived):
        if pairs[0][0] < pairs[0][1]:
            return value + arrived
        return jnp.where((place == pairs[0][1]) | (place == pairs[1][1]), arrived, value)

    return arrived, combine


def region(run, *operands):
    results = jax.eval_shape(run, *operands)

    def nothing(*_):
        return jax.tree.map(lambda one: jnp.zeros(one.shape, one.dtype), results)

    return lax.cond(lax.axis_index("col") >= 0, run, nothing, *operands)


def together(*values):
    return lax.optimization_barrier(values)


def body(window, reflectors, factors):
    row_count = lax.axis_size("row")
    chips = lax.axis_size("col") // 2
    row, chip = lax.axis_index("row"), lax.axis_index("col") // 2
    lower = chip < chips // 2
    rows, cols = window.shape
    panels = reflectors.shape[0]
    bits = [1 << bit for bit in range(row_count.bit_length() - 1)]
    orders = [bits[::-1] if panel % 2 else bits for panel in range(panels)]
    slivers = jnp.swapaxes(reflectors, 1, 2)
    near, held, ends, columns, (near_projected, same), images = gather_vectors(
        slivers, row_count, chips, window
    )
    part = near.shape[0] // panels
    width = 2 * part
    total = panels * width
    near_parts = [near_projected[part * panel : part * (panel + 1)] for panel in range(panels)]
    steps = [scatter_step(one, order[0]) for one, order in zip(near_parts, orders)]
    last_columns, *images = together(columns[-1], *images)
    last_image, ends, *arrived = together(
        image(window, last_columns), ends, *[one for one, _ in steps]
    )
    held[chips - 1], held[1 - chips] = ends, ends
    half = chips // 2
    far = [
        by_chip(lambda one: held[(1 - one // half) * half + place - one]) for place in range(half)
    ]
    images.append(last_image)
    near_parts = [one + kept for one, (_, kept) in zip(arrived, steps)]
    summed = [lax.psum(one, "col") for one in images]
    columns = jnp.concatenate(columns, 0)

    def factors_of(window, near, far, same, columns, factors, images, near_parts):
        far = both_cores(far, [swap_cores(one) for one in far])
        crossed = cross(near, far, images)
        crossed = ordered(lower, crossed[: total // 2], crossed[total // 2 :], 0)
        sums = [crossed[: total // 2], crossed[total // 2 :]]
        steps = [scatter_step(one, order[0]) for one, order in zip(sums, (bits, bits[::-1]))]
        near_steps = [scatter_step(one, order[1]) for one, order in zip(near_parts, orders)]
        (far_projected, opposite, crossing, mixed), arrived, near_arrived = together(
            project([far, near], window, [(0, 0), (0, 1), (1, 0)]),
            [one for one, _ in steps],
            [one for one, _ in near_steps],
        )
        sums = [one + kept for one, (_, kept) in zip(arrived, steps)]
        near_parts = [one + kept for one, (_, kept) in zip(near_arrived, near_steps)]
        for step in range(2, len(bits)):
            steps = [scatter_step(one, order[step]) for one, order in zip(near_parts, orders)]
            near_parts = [one + kept for one, kept in steps]
        far_parts = [far_projected[part * panel : part * (panel + 1)] for panel in range(panels)]
        for step in range(len(bits)):
            far_steps = [scatter_step(one, order[step]) for one, order in zip(far_parts, orders)]
            steps = []
            if step + 1 < len(bits):
                steps = [
                    scatter_step(one, order[step + 1])
                    for one, order in zip(sums, (bits, bits[::-1]))
                ]
            else:
                crossed = jnp.concatenate(sums, 0)
                steps = [(swap_cores(crossed), crossed)]
            arrived, far_arrived = together([one for one, _ in steps], [one for one, _ in far_steps])
            sums = [one + kept for one, (_, kept) in zip(arrived, steps)]
            far_parts = [one + kept for one, (_, kept) in zip(far_arrived, far_steps)]
        (crossed,) = sums

        def of(value, one, two):
            return value[part * one : part * (one + 1), part * two : part * (two + 1)]

        inner = [
            ordered(
                lower,
                ordered(lower, of(same, one, two), of(mixed, one, two), 1),
                ordered(lower, of(crossing, one, two), of(opposite, one, two), 1),
                0,
            )
            for one in range(panels)
            for two in range(one + 1, panels)
        ]
        parts = [jnp.stack([one, two]) for one, two in zip(near_parts, far_parts)]
        hops = chips - 1
        for step, bit in enumerate(bits):
            others = [swap_rows(one, bit) for one in inner]
            parts = [gather_step(one, order[-1 - step]) for one, order in zip(parts, orders)]
            if step < hops:
                arrived, combine = line_step(crossed, step, chips)
                parts, others, arrived = together(parts, others, arrived)
                crossed = combine(crossed, arrived)
            else:
                parts, others = together(parts, others)
            inner = [one + two for one, two in zip(inner, others)]
        projected = jnp.concatenate(parts, 0).reshape(total, cols)

        for hop in range(len(bits), hops - 1):
            arrived, combine = line_step(crossed, hop, chips)
            crossed = combine(crossed, arrived)
        local, left, *right = prepare(lower, projected, columns, factors, inner)
        if len(bits) < hops:
            arrived, combine = line_step(crossed, hops - 1, chips)
            arrived, local, left, right = together(arrived, local, left, right)
            crossed = combine(crossed, arrived)
        everyone = [crossed] + [swap_rows(crossed, distance) for distance in range(1, row_count)]
        crossed = jnp.zeros((2, total // 2, total), f32)
        for distance, value in enumerate(everyone):
            source = row ^ distance
            for other, order in enumerate((bits, bits[::-1])):
                place, size = 0, total // 2
                for bit in order:
                    size = size // 2
                    place = place + (source // bit) % 2 * size
                crossed = lax.dynamic_update_slice(
                    crossed, value[other * size : (other + 1) * size][None], (other, place, 0)
                )
        crossed = crossed.reshape(2, panels, part, total)
        crossed = jnp.concatenate(
            [crossed[other, panel] for panel in range(panels) for other in range(2)], 0
        )
        return far, *weights(local, crossed, left, right)

    far, high, low = region(
        factors_of, window, near, far, same, columns, factors, images, near_parts
    )
    return finish(window, near, far, high, low, summed)


def solution(mesh):
    placed = (P("row", "col"), P(None, "row", "col"), P())
    return jax.shard_map(
        body, mesh=mesh, in_specs=placed, out_specs=P("row", "col"), check_vma=False
    )
```

```python
import functools

import jax
import jax.numpy as jnp
from jax import lax
from jax.experimental import pallas as pl
from jax.experimental.pallas import tpu as pltpu
from jax.sharding import PartitionSpec as P

f32 = jnp.float32
bf16 = jnp.bfloat16
MIB = 1024 * 1024


def halves(value):
    high = value.astype(bf16)
    return high, (value - high.astype(f32)).astype(bf16)


def dot(one, two, one_dim=1, two_dim=0):
    return lax.dot_general(
        one, two, (((one_dim,), (two_dim,)), ((), ())), preferred_element_type=f32
    )


def small(one, two, one_dim=1, two_dim=0):
    return lax.dot_general(
        one,
        two,
        (((one_dim,), (two_dim,)), ((), ())),
        precision=lax.Precision.HIGH,
        preferred_element_type=f32,
    )


def call(kernel, mebibytes, grid, in_specs, out_specs, out_shape, scratch=()):
    return pl.pallas_call(
        kernel,
        grid=grid,
        in_specs=in_specs,
        out_specs=out_specs,
        out_shape=out_shape,
        scratch_shapes=scratch,
        compiler_params=pltpu.CompilerParams(vmem_limit_bytes=mebibytes * MIB),
        cost_estimate=pl.CostEstimate(flops=1, bytes_accessed=1, transcendentals=0),
    )


def three_products(one, two, one_dim=1, two_dim=0):
    (high, low), (other_high, other_low) = one, two
    return dot(high, other_high, one_dim, two_dim) + (
        dot(high, other_low, one_dim, two_dim) + dot(low, other_high, one_dim, two_dim)
    )


def project_kernel(pairs, count, *refs):
    vectors_refs, (window_ref, out_ref) = refs[:count], refs[count : count + 2]
    products_refs, both_ref = refs[count + 2 : -1], refs[-1]
    width = out_ref.shape[0]

    @pl.when(pl.program_id(0) == 0)
    def _():
        values = [halves(ref[...]) for ref in vectors_refs]
        both_ref[:width], both_ref[width:] = values[0]
        for (one, two), ref in zip(pairs, products_refs):
            ref[...] = three_products(values[one], values[two], 1, 1)

    high, low = halves(window_ref[...])
    first = dot(both_ref[...], high)
    out_ref[...] = first[:width] + first[width:] + dot(both_ref[:width], low)


def project(vectors, window, pairs, block=256):
    width, rows = vectors[0].shape
    cols = window.shape[1]
    return call(
        functools.partial(project_kernel, pairs, len(vectors)),
        36,
        (cols // block,),
        [pl.BlockSpec((width, rows), lambda i: (0, 0))] * len(vectors)
        + [pl.BlockSpec((rows, block), lambda i: (0, i))],
        [pl.BlockSpec((width, block), lambda i: (0, i))]
        + [pl.BlockSpec((width, width), lambda i: (0, 0))] * len(pairs),
        [jax.ShapeDtypeStruct((width, cols), f32)]
        + [jax.ShapeDtypeStruct((width, width), f32)] * len(pairs),
        [pltpu.VMEM((2 * width, rows), bf16)],
    )(*vectors, window)


def image_kernel(window_ref, vectors_ref, out_ref, both_ref):
    width = vectors_ref.shape[0]

    @pl.when(pl.program_id(0) == 0)
    def _():
        high, low = halves(vectors_ref[...])
        both_ref[:width] = high
        both_ref[width:] = low

    high, low = halves(window_ref[...])
    first = dot(high, both_ref[...], 1, 1)
    out_ref[...] = first[:, :width] + first[:, width:] + dot(low, both_ref[:width], 1, 1)


def image(window, vectors, block=512):
    rows, cols = window.shape
    width = vectors.shape[0]
    block = min(block, rows)
    return call(
        image_kernel,
        22,
        (rows // block,),
        [
            pl.BlockSpec((block, cols), lambda i: (i, 0)),
            pl.BlockSpec((width, cols), lambda i: (0, 0)),
        ],
        pl.BlockSpec((block, width), lambda i: (i, 0)),
        jax.ShapeDtypeStruct((rows, width), f32),
        [pltpu.VMEM((2 * width, cols), bf16)],
    )(window, vectors)


def cross_kernel(near_ref, far_ref, *refs):
    *image_refs, out_ref = refs

    @pl.when(pl.program_id(0) == 0)
    def _():
        out_ref[...] = jnp.zeros_like(out_ref)

    vectors = jnp.concatenate([near_ref[...], far_ref[...]], 0)
    images = jnp.concatenate([one[...] for one in image_refs], 1)
    out_ref[...] += three_products(halves(vectors), halves(images))


def cross(near, far, images, block=512):
    part, rows = near.shape
    block = min(block, rows)
    width = sum(one.shape[1] for one in images)
    return call(
        cross_kernel,
        16,
        (rows // block,),
        [pl.BlockSpec((part, block), lambda i: (0, i))] * 2
        + [pl.BlockSpec((block, one.shape[1]), lambda i: (i, 0)) for one in images],
        pl.BlockSpec((2 * part, width), lambda i: (0, 0)),
        jax.ShapeDtypeStruct((2 * part, width), f32),
    )(near, far, *images)


def prepare_kernel(panels, lower_ref, projected_ref, columns_ref, factors_ref, *refs):
    *inner_refs, local_ref, left_ref, high_ref, low_ref = refs
    lower = lower_ref[0] == 1
    width = factors_ref.shape[1]
    part = width // 2
    joined = factors_ref[0]
    for panel in range(1, panels):
        done = panel * width
        inner = [
            inner_refs[one * (panels - 1) - one * (one - 1) // 2 + panel - one - 1][...]
            for one in range(panel)
        ]
        inner = jnp.concatenate(inner, 0) if panel > 1 else inner[0]
        factor = factors_ref[panel]
        between = three_products(halves(inner), halves(factor))
        between = -three_products(halves(joined), halves(between))
        joined = jnp.concatenate(
            [
                jnp.concatenate([joined, between], 1),
                jnp.concatenate([jnp.zeros((width, done), f32), factor], 1),
            ],
            0,
        )

    def chosen(value, panel, other, dim):
        start = panel * width
        one = lax.slice_in_dim(value, start, start + part, axis=dim)
        two = lax.slice_in_dim(value, start + part, start + width, axis=dim)
        return jnp.where(lower == (other == 0), one, two)

    local = jnp.concatenate(
        [chosen(joined, panel, other, 1) for other in range(2) for panel in range(panels)], 1
    )
    both = jnp.concatenate(
        [chosen(local, panel, other, 0) for panel in range(panels) for other in range(2)], 0
    )
    local_ref[...] = local
    left_ref[...] = three_products(halves(both), halves(projected_ref[...]), 0, 0)
    high_ref[...], low_ref[...] = halves(
        three_products(halves(joined), halves(columns_ref[...]))
    )


def prepare(lower, projected, columns, factors, inner):
    total, cols = projected.shape
    return call(
        functools.partial(prepare_kernel, factors.shape[0]),
        36,
        (),
        [pl.BlockSpec(memory_space=pltpu.SMEM)]
        + [pl.BlockSpec(memory_space=pltpu.VMEM)] * (3 + len(inner)),
        [pl.BlockSpec(memory_space=pltpu.VMEM)] * 4,
        [
            jax.ShapeDtypeStruct((total, total), f32),
            jax.ShapeDtypeStruct((total, cols), f32),
            jax.ShapeDtypeStruct((total, cols), bf16),
            jax.ShapeDtypeStruct((total, cols), bf16),
        ],
    )(lower.astype(jnp.int32).reshape(1), projected, columns, factors, *inner)


def weights_kernel(
    local_ref, crossed_ref, left_ref, right_high, right_low, high_ref, low_ref
):
    width = left_ref.shape[0]
    middle = three_products(halves(local_ref[...]), halves(crossed_ref[...]), 0, 0)
    left = left_ref[...] - three_products(halves(middle), (right_high[...], right_low[...]))
    high_ref[:width], low_ref[:width] = halves(left)
    high_ref[width:], low_ref[width:] = right_high[...], right_low[...]


def weights(local, crossed, left, right):
    width, cols = left.shape
    return call(
        weights_kernel,
        30,
        (),
        [pl.BlockSpec(memory_space=pltpu.VMEM)] * 5,
        [pl.BlockSpec(memory_space=pltpu.VMEM)] * 2,
        [jax.ShapeDtypeStruct((2 * width, cols), bf16)] * 2,
    )(local, crossed, left, *right)


def finish_kernel(window_ref, near_ref, far_ref, high_ref, low_ref, *refs):
    *image_refs, out_ref = refs
    both = jnp.concatenate(
        [near_ref[...].T, far_ref[...].T] + [one[...] for one in image_refs], 1
    )
    out_ref[...] = window_ref[...] - three_products(halves(both), (high_ref[...], low_ref[...]))


def finish(window, near, far, high, low, images, block=512):
    rows, cols = window.shape
    part, width = near.shape[0], high.shape[0]
    block = min(block, rows)
    return call(
        finish_kernel,
        52,
        (rows // block,),
        [
            pl.BlockSpec((block, cols), lambda i: (i, 0)),
            pl.BlockSpec((part, block), lambda i: (0, i)),
            pl.BlockSpec((part, block), lambda i: (0, i)),
        ]
        + [pl.BlockSpec((width, cols), lambda i: (0, 0))] * 2
        + [pl.BlockSpec((block, one.shape[1]), lambda i: (i, 0)) for one in images],
        pl.BlockSpec((block, cols), lambda i: (i, 0)),
        jax.ShapeDtypeStruct((rows, cols), f32),
    )(window, near, far, high, low, *images)


def swap_cores(value):
    count = lax.axis_size("col")
    return lax.ppermute(value, "col", [(col, col ^ 1) for col in range(count)])


def swap_chips(value, distance):
    count = lax.axis_size("col")
    return lax.ppermute(value, "col", [(col, col ^ (2 * distance)) for col in range(count)])


def swap_rows(value, distance):
    count = lax.axis_size("row")
    return lax.ppermute(value, "row", [(row, row ^ distance) for row in range(count)])


def at(value, index, dim):
    return lax.dynamic_index_in_dim(value, index, dim, keepdims=False)


def put(whole, value, index, dim):
    return lax.dynamic_update_slice_in_dim(whole, jnp.expand_dims(value, dim), index, dim)


def together(*values):
    return lax.optimization_barrier(values)


def region(run, *operands):
    results = jax.eval_shape(run, *operands)

    def nothing(*_):
        return jax.tree.map(lambda one: jnp.zeros(one.shape, one.dtype), results)

    return lax.cond(lax.axis_index("col") >= 0, run, nothing, *operands)


def ordered(condition, one, two, dim):
    return jnp.concatenate([jnp.where(condition, one, two), jnp.where(condition, two, one)], dim)


def by_chip(choose):
    chip = lax.axis_index("col") // 2
    value = choose(0)
    for one in range(1, lax.axis_size("col") // 2):
        value = jnp.where(chip == one, choose(one), value)
    return value


def send_along(value, chips, step, count=None):
    count = chips if count is None else count
    ends = range(count) if step < 0 else range(chips - count, chips)
    return lax.ppermute(
        value,
        "col",
        [
            (2 * (chip - step) + core, 2 * chip + core)
            for chip in ends
            for core in range(2)
            if 0 <= chip - step < chips
        ],
    )


def both_cores(mine, other):
    core = lax.axis_index("col") % 2
    pairs = []
    for one, two in zip(mine, other):
        pairs += [jnp.where(core == 0, one, two), jnp.where(core == 0, two, one)]
    return jnp.concatenate(pairs, 1).reshape(-1, mine[0].shape[-1])


def gather_vectors(slivers, row_count, chips, window):
    col_index, row = lax.axis_index("col"), lax.axis_index("row")
    core, chip = col_index % 2, col_index // 2
    panels, piece, rows = slivers.shape
    cols = rows // 2
    share = 2 * piece // row_count
    distances = range(1, row_count)
    half = chips // 2

    mine = lax.dynamic_slice_in_dim(slivers, core * cols, cols, 2)
    other = swap_cores(lax.dynamic_slice_in_dim(slivers, (1 - core) * cols, cols, 2))
    shares = ordered(core == 0, mine, other, 1).reshape(panels, row_count, share, cols)
    arrived = [swap_rows(at(shares, row ^ distance, 1), distance) for distance in distances]
    held = {0: slivers}
    for step in range(1, half):
        after, before, *arrived = together(
            send_along(held[step - 1], chips, -1), send_along(held[1 - step], chips, 1), *arrived
        )
        held[step], held[-step] = after, before
    by_row = jnp.zeros((panels, row_count, share, cols), f32)
    by_row = put(by_row, at(shares, row, 1), row, 1)
    for distance, value in zip(distances, arrived):
        by_row = put(by_row, value, row ^ distance, 1)

    near = jnp.stack(
        [by_chip(lambda one: held[one // half * half + place - one]) for place in range(half)], 1
    )

    def along_line(panel):
        return [swap_chips(at(by_row[panel], chip ^ distance, 0), distance) for distance in distances]

    def line_shares(panel, arrived):
        shares = jnp.zeros((row_count, share, cols), f32)
        shares = put(shares, at(by_row[panel], chip, 0), chip, 0)
        for distance, value in zip(distances, arrived):
            shares = put(shares, value, chip ^ distance, 0)
        return shares

    def all_rows(shares, arrived):
        whole = jnp.zeros((row_count, row_count, share, cols), f32)
        whole = put(whole, shares, row, 1)
        for distance, value in zip(distances, arrived):
            whole = put(whole, value, row ^ distance, 1)
        return whole.reshape(2 * chips * piece, cols)

    other, arrived = together(swap_cores(near), along_line(0))
    near, other = (
        [value[:, place] for place in range(half)] for value in (near, other)
    )
    near = both_cores(near, other)
    shares = [line_shares(0, arrived)]
    last = (held[half - 1], held[1 - half])
    *last, near, shares[0] = together(*last, near, shares[0])

    columns, images = [], []
    for panel in range(panels):
        arrived = [swap_rows(shares[panel], distance) for distance in distances]
        following = along_line(panel + 1) if panel + 1 < panels else []
        if panel == 0:
            projected, arrived, following = together(project([near], window, [(0, 0)]), arrived, following)
        else:
            jumps = range(1, half)
            after = [send_along(last[0], chips, -jump, chips - half - jump + 1) for jump in jumps]
            before = [send_along(last[1], chips, jump, chips - half - jump + 1) for jump in jumps]
            images.append(image(window, columns[-1]))
            images[-1], arrived, following, after, before = together(
                images[-1], arrived, following, after, before
            )
            for jump, one, two in zip(jumps, after, before):
                held[half - 1 + jump], held[1 - half - jump] = one, two
        columns.append(all_rows(shares[panel], arrived))
        if following:
            shares.append(line_shares(panel + 1, following))
    ends = lax.ppermute(
        jnp.where(chip < half, last[1], last[0]),
        "col",
        [
            (2 * one + which, 2 * two + which)
            for one, two in ((half, 0), (half - 1, chips - 1))
            for which in range(2)
        ],
    )
    return near, held, ends, columns, projected, images


def scatter_step(value, bit):
    half = value.shape[0] // 2
    upper = (lax.axis_index("row") // bit) % 2
    sent = lax.dynamic_slice_in_dim(value, (1 - upper) * half, half, 0)
    kept = lax.dynamic_slice_in_dim(value, upper * half, half, 0)
    return swap_rows(sent, bit), kept


def gather_step(value, bit):
    upper = (lax.axis_index("row") // bit) % 2
    return ordered(upper == 0, value, swap_rows(value, bit), 1)


def line_step(value, hop, chips):
    middle = chips // 2
    place = lax.axis_index("col") // 2
    if hop < middle:
        pairs = [(hop, hop + 1), (chips - 1 - hop, chips - 2 - hop)]
    else:
        hop = chips - 2 - hop
        pairs = [(hop + 1, hop), (chips - 2 - hop, chips - 1 - hop)]
    arrived = lax.ppermute(
        value, "col", [(2 * one + core, 2 * two + core) for one, two in pairs for core in range(2)]
    )

    def combine(value, arrived):
        if pairs[0][0] < pairs[0][1]:
            return value + arrived
        return jnp.where((place == pairs[0][1]) | (place == pairs[1][1]), arrived, value)

    return arrived, combine


def region(run, *operands):
    results = jax.eval_shape(run, *operands)

    def nothing(*_):
        return jax.tree.map(lambda one: jnp.zeros(one.shape, one.dtype), results)

    return lax.cond(lax.axis_index("col") >= 0, run, nothing, *operands)


def together(*values):
    return lax.optimization_barrier(values)


def body(window, reflectors, factors):
    row_count = lax.axis_size("row")
    chips = lax.axis_size("col") // 2
    row, chip = lax.axis_index("row"), lax.axis_index("col") // 2
    lower = chip < chips // 2
    core = lax.axis_index("col") % 2
    rows, cols = window.shape
    panels = reflectors.shape[0]
    bits = [1 << bit for bit in range(row_count.bit_length() - 1)]
    orders = [bits[::-1] if panel % 2 else bits for panel in range(panels)]
    slivers = jnp.swapaxes(reflectors, 1, 2)
    near, held, ends, columns, (near_projected, same), images = gather_vectors(
        slivers, row_count, chips, window
    )
    part = near.shape[0] // panels
    width = 2 * part
    total = panels * width
    near_parts = [near_projected[part * panel : part * (panel + 1)] for panel in range(panels)]
    steps = [scatter_step(one, order[0]) for one, order in zip(near_parts, orders)]
    last_columns, *images = together(columns[-1], *images)
    last_image, ends, *arrived = together(
        image(window, last_columns), ends, *[one for one, _ in steps]
    )
    held[chips - 1], held[1 - chips] = ends, ends
    half = chips // 2
    far = [
        by_chip(lambda one: held[(1 - one // half) * half + place - one]) for place in range(half)
    ]
    images.append(last_image)
    near_parts = [one + kept for one, (_, kept) in zip(arrived, steps)]
    summed = [lax.psum(one, "col") for one in images]
    columns = jnp.concatenate(columns, 0)

    def factors_of(window, near, far, same, columns, factors, images, near_parts):
        far = both_cores(far, [swap_cores(one) for one in far])
        crossed = cross(near, far, images)
        crossed = ordered(lower, crossed[: total // 2], crossed[total // 2 :], 0)
        sums = [crossed[: total // 2], crossed[total // 2 :]]
        steps = [scatter_step(one, order[0]) for one, order in zip(sums, (bits, bits[::-1]))]
        near_steps = [scatter_step(one, order[1]) for one, order in zip(near_parts, orders)]
        (far_projected, opposite, crossing, mixed), arrived, near_arrived = together(
            project([far, near], window, [(0, 0), (0, 1), (1, 0)]),
            [one for one, _ in steps],
            [one for one, _ in near_steps],
        )
        sums = [one + kept for one, (_, kept) in zip(arrived, steps)]
        near_parts = [one + kept for one, (_, kept) in zip(near_arrived, near_steps)]
        for step in range(2, len(bits)):
            steps = [scatter_step(one, order[step]) for one, order in zip(near_parts, orders)]
            near_parts = [one + kept for one, kept in steps]
        far_parts = [far_projected[part * panel : part * (panel + 1)] for panel in range(panels)]
        def of(value, one, two):
            return value[part * one : part * (one + 1), part * two : part * (two + 1)]

        inner = [
            ordered(
                lower,
                ordered(lower, of(same, one, two), of(mixed, one, two), 1),
                ordered(lower, of(crossing, one, two), of(opposite, one, two), 1),
                0,
            )
            for one in range(panels)
            for two in range(one + 1, panels)
        ]
        for step in range(len(bits)):
            far_steps = [scatter_step(one, order[step]) for one, order in zip(far_parts, orders)]
            steps = []
            if step + 1 < len(bits):
                steps = [
                    scatter_step(one, order[step + 1])
                    for one, order in zip(sums, (bits, bits[::-1]))
                ]
            else:
                crossed = jnp.concatenate(sums, 0)
                half = crossed.shape[0] // 2
                sent = lax.dynamic_slice_in_dim(crossed, (1 - core) * half, half, 0)
                kept = lax.dynamic_slice_in_dim(crossed, core * half, half, 0)
                steps = [(swap_cores(sent), kept)]
            others = [swap_rows(one, bits[step - 1]) for one in inner] if step else []
            arrived, far_arrived, others = together(
                [one for one, _ in steps], [one for one, _ in far_steps], others
            )
            inner = [one + two for one, two in zip(inner, others)] if step else inner
            sums = [one + kept for one, (_, kept) in zip(arrived, steps)]
            far_parts = [one + kept for one, (_, kept) in zip(far_arrived, far_steps)]
        (crossed,) = sums

        parts = [jnp.stack([one, two]) for one, two in zip(near_parts, far_parts)]
        hops = chips - 1
        for step in range(len(bits)):
            others = [swap_rows(one, bits[-1]) for one in inner] if step == 0 else []
            parts = [gather_step(one, order[-1 - step]) for one, order in zip(parts, orders)]
            if step < hops:
                arrived, combine = line_step(crossed, step, chips)
                parts, others, arrived = together(parts, others, arrived)
                crossed = combine(crossed, arrived)
            else:
                parts, others = together(parts, others)
            inner = [one + two for one, two in zip(inner, others)] if step == 0 else inner
        projected = jnp.concatenate(parts, 0).reshape(total, cols)

        for hop in range(len(bits), hops - 1):
            arrived, combine = line_step(crossed, hop, chips)
            crossed = combine(crossed, arrived)
        local, left, *right = prepare(lower, projected, columns, factors, inner)
        if len(bits) < hops:
            arrived, combine = line_step(crossed, hops - 1, chips)
            arrived, local, left, right = together(arrived, local, left, right)
            crossed = combine(crossed, arrived)
        everyone = [crossed] + [swap_rows(crossed, distance) for distance in range(1, row_count)]
        others = swap_cores(jnp.stack(everyone))
        everyone = [ordered(core == 0, one, others[place], 0) for place, one in enumerate(everyone)]
        crossed = jnp.zeros((2, total // 2, total), f32)
        for distance, value in enumerate(everyone):
            source = row ^ distance
            for other, order in enumerate((bits, bits[::-1])):
                place, size = 0, total // 2
                for bit in order:
                    size = size // 2
                    place = place + (source // bit) % 2 * size
                crossed = lax.dynamic_update_slice(
                    crossed, value[other * size : (other + 1) * size][None], (other, place, 0)
                )
        crossed = crossed.reshape(2, panels, part, total)
        crossed = jnp.concatenate(
            [crossed[other, panel] for panel in range(panels) for other in range(2)], 0
        )
        return far, *weights(local, crossed, left, right)

    far, high, low = region(
        factors_of, window, near, far, same, columns, factors, images, near_parts
    )
    return finish(window, near, far, high, low, summed)


def solution(mesh):
    placed = (P("row", "col"), P(None, "row", "col"), P())
    return jax.shard_map(
        body, mesh=mesh, in_specs=placed, out_specs=P("row", "col"), check_vma=False
    )
```
